32 devices in a mesh: wa: 8 (over z, y), dev: 4 (over x, core).
Axes of the slice: x: 2, y: 2, z: 4, core: 2. Of those that a mesh axis runs over, the one named last changes fastest.
Arguments:
- output_gradient: bfloat16 [1024, 8192], P('wa'), may hold values from -6 to 6
- down_weight: bfloat16 [28672, 8192], P('dev', 'wa'), may hold values from -0.03125 to 0.03125
- gate_preactivation: bfloat16 [1024, 28672], P('wa', 'dev'), may hold values from -6 to 6
- up_preactivation: bfloat16 [1024, 28672], P('wa', 'dev'), may hold values from -6 to 6
- adapter_down_factor: bfloat16 [16, 16, 28672], P(None, None, 'dev'), may hold values from -0.0625 to 0.0625
- adapter_up_factor: bfloat16 [16, 16, 8192], P(None, None, 'dev'), may hold values from -0.0625 to 0.0625
- tile_owner_adapter: int32 [64, 1], replicated, may hold values from 0 to 15
- tile_live_count: int32 [64], replicated, may hold values from 1 to 16
Outputs:
- grad_gate: bfloat16 [1024, 28672], P('wa', 'dev')
- grad_up: bfloat16 [1024, 28672], P('wa', 'dev')
- grad_a: float32 [16, 16, 28672], P('wa', None, 'dev')
- grad_b: float32 [16, 16, 8192], P('wa', None, 'dev')
The draws below stay inside these ranges and needn't reach their ends.
Inputs may be any that keep to these rules, and one draw needn't show every extreme that they name: `tile_owner_adapter`: every one of the 16 adapters owns at least one tile.
All inputs are finite; a program needn't handle non-finite values.
Results may differ from the reference program's by a relative error of at most 0.013.
Values may be sent and summed in bfloat16 or wider, within the bound.
No kernel may reach another device: no remote copies, remote signals or barrier semaphores. Data moves between devices by JAX's collectives and lax.ppermute only.
A program may use at most 128 MiB of HBM per device.

```python
import jax
import jax.numpy as jnp
from jax import lax

MODEL_WIDTH = 8192
HIDDEN_UNITS = 28672
ADAPTER_RANK = 16
ADAPTER_COUNT = 16
TILE = 16
TOKENS = 1024
TILES = 64
N_WA = 8


def set_ends(drawn, rng, least, high):
    spot = [jax.random.randint(jax.random.fold_in(rng, axis), (), 0, length) for axis, length in enumerate(drawn.shape)]
    widest = drawn.shape.index(max(drawn.shape))
    next_to = spot[:widest] + [(spot[widest] + 1) % drawn.shape[widest]] + spot[widest + 1:]
    return drawn.at[tuple(spot)].set(least).at[tuple(next_to)].set(high)


def spiked(values, rng, source, target, shards_of, factor):
    owner, partner = [(jnp.arange(values.shape[axis_at]) // (values.shape[axis_at] // shards_of)).reshape([-1 if axis == axis_at else 1 for axis in range(values.ndim)]) for axis_at in (source, target)]
    chosen = jax.random.permutation(rng, shards_of)[partner]
    strong = (owner == chosen) | (owner == (partner + shards_of // 2) % shards_of)
    return jnp.where(strong, factor * values, values)


def block_levels(rng, extent, shards, low, high):
    level = 1.0
    for axis_at, shards_of in shards:
        heights = jax.random.uniform(jax.random.fold_in(jax.random.fold_in(rng, 6), axis_at), (shards_of,), jnp.float32, low / len(shards), high / len(shards))
        level = level * jnp.repeat(jnp.exp(heights), extent[axis_at] // shards_of).reshape((-1,) + (1,) * (len(extent) - 1 - axis_at))
    return level


def choose_distinct(own_key, rows, number_of, top, lift):
    sequence = jax.random.permutation(jax.random.fold_in(own_key, 1), number_of)
    favour = sequence
    for power in range(3):
        favour = favour * favour // number_of
    favour = favour * lift // number_of
    lots = jax.random.randint(jax.random.fold_in(own_key, 2), (rows, number_of), 0, 4096) + favour
    holders = jax.random.permutation(jax.random.fold_in(own_key, 3), rows)[jnp.arange(number_of) % rows]
    lots = jnp.where(jnp.arange(rows)[:, None] == holders[None, :], 1 << 14, lots)
    score = lots * number_of + jnp.arange(number_of)
    return lax.top_k(score.astype(jnp.int32), top)[1].astype(jnp.int32)


def bell_draw(own_key, extent, scale, reach, pieces=(), kind=jnp.bfloat16):
    entries = jax.random.normal(own_key, extent, jnp.float32) * scale
    if len(pieces) > 0:
        entries = block_levels(own_key, extent, pieces, -0.22, 0.18) * entries
    return jnp.clip(entries, min=-reach, max=reach).astype(kind)


def gaussian_with(own_key, dims, spread, reach, pieces, heavy, kind=jnp.bfloat16):
    values = spread * jax.random.normal(own_key, dims, jnp.float32)
    if pieces:
        values = values * block_levels(own_key, dims, pieces, -0.22, 0.18)
    return jnp.clip(spiked(values, jax.random.fold_in(own_key, 3), *heavy), -reach, reach).astype(kind)


def setup_inputs(seed: int = 0) -> dict:
    seeds = jax.random.split(jax.random.key(seed), 9)
    output_gradient = gaussian_with(seeds[0], (TOKENS, MODEL_WIDTH), 1.0, 6.0, ((0, 8),), (1, 0, 8, 2.0))
    down_weight = bell_draw(seeds[1], (HIDDEN_UNITS, MODEL_WIDTH), HIDDEN_UNITS ** -0.5, 0.03125, ((0, 4), (1, 8)))
    gate_preactivation = bell_draw(seeds[2], (TOKENS, HIDDEN_UNITS), 1.0, 6.0, ((0, 8), (1, 4)))
    up_preactivation = bell_draw(seeds[3], (TOKENS, HIDDEN_UNITS), 1.0, 6.0, ((0, 8), (1, 4)))
    adapter_down_factor = bell_draw(seeds[4], (ADAPTER_COUNT, ADAPTER_RANK, HIDDEN_UNITS), (HIDDEN_UNITS // 4) ** -0.5, 0.0625, ((2, 4),))
    adapter_up_factor = bell_draw(seeds[5], (ADAPTER_COUNT, ADAPTER_RANK, MODEL_WIDTH), MODEL_WIDTH ** -0.5, 0.0625, ((2, 4),))
    tile_owner_adapter = choose_distinct(seeds[6], TILES, ADAPTER_COUNT, 1, 1024)
    tile_live_count = set_ends(jax.random.randint(seeds[7], (TILES,), 1, TILE + 1), jax.random.fold_in(seeds[7], 1), 1, TILE).astype(jnp.int32)
    return dict(output_gradient=output_gradient, down_weight=down_weight, gate_preactivation=gate_preactivation, up_preactivation=up_preactivation, adapter_down_factor=adapter_down_factor, adapter_up_factor=adapter_up_factor, tile_owner_adapter=tile_owner_adapter, tile_live_count=tile_live_count)


def reference(output_gradient, down_weight, gate_preactivation, up_preactivation, adapter_down_factor, adapter_up_factor, tile_owner_adapter, tile_live_count):
    row_adapter = jnp.repeat(tile_owner_adapter[:, 0], TILE)
    position = (jnp.arange(TOKENS) % TILE).astype(jnp.int32)
    live_rows = position < jnp.repeat(tile_live_count, TILE)
    masked_rows = jnp.where(live_rows[:, None], output_gradient, jnp.zeros((), output_gradient.dtype))
    gate_wide = gate_preactivation.astype(jnp.float32)
    up_wide = up_preactivation.astype(jnp.float32)
    hidden_state = (jax.nn.silu(gate_wide) * up_wide).astype(jnp.bfloat16)
    group_width = MODEL_WIDTH // N_WA

    def add_group(group_number, running):
        offset = (group_number * group_width).astype(jnp.int32)
        columns = lax.dynamic_slice_in_dim(masked_rows, offset, group_width, 1)
        weights = lax.dynamic_slice_in_dim(down_weight, offset, group_width, 1)
        partial_value = lax.dot_general(columns, weights, (((1,), (1,)), ((), ())), preferred_element_type=jnp.float32)
        rounded = lax.optimization_barrier(partial_value.astype(jnp.bfloat16))
        return running + rounded.astype(jnp.float32)

    base_grad = lax.fori_loop(0, N_WA, add_group, jnp.zeros((TOKENS, HIDDEN_UNITS), jnp.float32))
    selector = row_adapter[:, None] == jnp.arange(ADAPTER_COUNT, dtype=jnp.int32)[None, :]
    flattened_down = adapter_down_factor.reshape(ADAPTER_COUNT * ADAPTER_RANK, HIDDEN_UNITS)
    flattened_up = adapter_up_factor.reshape(ADAPTER_COUNT * ADAPTER_RANK, MODEL_WIDTH)

    def choose_rows(complete_value):
        reshaped_value = complete_value.reshape(TOKENS, ADAPTER_COUNT, ADAPTER_RANK)
        return jnp.sum(jnp.where(selector[:, :, None], reshaped_value, jnp.zeros((), complete_value.dtype)), axis=1)

    def spread_value(values):
        wide_value = jnp.where(selector[:, :, None], values[:, None, :], jnp.zeros((), values.dtype))
        return wide_value.reshape(TOKENS, ADAPTER_COUNT * ADAPTER_RANK)

    adapter_input = choose_rows(lax.dot_general(hidden_state, flattened_down, (((1,), (1,)), ((), ())), preferred_element_type=jnp.float32)).astype(jnp.bfloat16)
    adapter_output = choose_rows(lax.dot_general(masked_rows, flattened_up, (((1,), (1,)), ((), ())), preferred_element_type=jnp.float32)).astype(jnp.bfloat16)
    spread_output = spread_value(adapter_output)
    spread_input = spread_value(adapter_input)
    hidden_grad = base_grad + 2.0 * jnp.dot(spread_output, flattened_down, preferred_element_type=jnp.float32)
    sigmoid_gate = jax.nn.sigmoid(gate_wide)
    grad_up = (hidden_grad * gate_wide * sigmoid_gate).astype(jnp.bfloat16)
    grad_gate = (hidden_grad * up_wide * sigmoid_gate * (1.0 + gate_wide * (1.0 - sigmoid_gate))).astype(jnp.bfloat16)
    grad_a = 2.0 * lax.dot_general(spread_output, hidden_state, (((0,), (0,)), ((), ())), preferred_element_type=jnp.float32)
    grad_b = 2.0 * lax.dot_general(spread_input, masked_rows, (((0,), (0,)), ((), ())), preferred_element_type=jnp.float32)
    return grad_gate, grad_up, grad_a.reshape(ADAPTER_COUNT, ADAPTER_RANK, HIDDEN_UNITS), grad_b.reshape(ADAPTER_COUNT, ADAPTER_RANK, MODEL_WIDTH)
```

```python
import jax
import jax.numpy as jnp
from jax import lax
from jax.sharding import PartitionSpec as P

TILE = 16
BF16 = jnp.bfloat16
F32 = jnp.float32


def nt_dot(left, right):
    return lax.dot_general(left, right, (((1,), (1,)), ((), ())), preferred_element_type=F32)


def tn_dot(left, right):
    return lax.dot_general(left, right, (((0,), (0,)), ((), ())), preferred_element_type=F32)


def ring_order(length):
    return [0] + list(range(1, length, 2)) + [z for z in range(length - 1, 0, -1) if z % 2 == 0]


class Group:
    def __init__(self, size):
        self.size = size
        self.length = size // 2
        self.order = ring_order(self.length)
        self.places = [(place, half) for place in range(self.length) for half in range(2)]

    def rank(self, place, half):
        return self.order[place % self.length] * 2 + half

    def swap_pairs(self):
        return [(w, w ^ 1) for w in range(self.size)]

    def next_pairs(self):
        return [(self.rank(p, h), self.rank(p + 1, h)) for p, h in self.places]

    def fetch_pairs(self, ahead, flip):
        return [(self.rank(p + ahead, h ^ flip), self.rank(p, h)) for p, h in self.places]

    def table(self, ahead, flip):
        entries = [0] * self.size
        for p, h in self.places:
            entries[self.rank(p, h)] = self.rank(p + ahead, h ^ flip)
        return entries


def add_round(first, second):
    return (first.astype(F32) + second.astype(F32)).astype(BF16)


def ring_sum(group, parts):
    travelling = parts[-1]
    for part in parts[-2::-1]:
        arrived = lax.ppermute(travelling, "wa", group.next_pairs())
        total = part.astype(F32) + arrived.astype(F32)
        travelling = total.astype(BF16)
    return total


def butterfly_sum(value, count):
    step = count // 2
    while step:
        value = value + lax.ppermute(value, "dev", [(d, d ^ step) for d in range(count)])
        step //= 2
    return value


def butterfly_gather(block, count):
    held = block[None]
    spans = [0]
    step = count // 2
    while step:
        other = lax.ppermute(held, "dev", [(d, d ^ step) for d in range(count)])
        held = jnp.concatenate([held, other], axis=0)
        spans = spans + [s ^ step for s in spans]
        step //= 2
    return [held[spans.index(j)] for j in range(count)], held, spans


def chunk_count(columns):
    for count in (7, 8, 4, 2):
        if columns % (128 * count) == 0:
            return count
    return 1


def run(
    rows,
    wa_size,
    dev_size,
    output_gradient,
    down_weight,
    gate_preactivation,
    up_preactivation,
    adapter_down_factor,
    adapter_up_factor,
    tile_owner_adapter,
    tile_live_count,
):
    group = Group(wa_size)
    length = group.length
    me = lax.axis_index("wa")
    dev = lax.axis_index("dev")
    token_rows, model_width = output_gradient.shape
    hidden_local = down_weight.shape[0]
    group_width = down_weight.shape[1]
    shard_columns = adapter_up_factor.shape[2]
    adapters, rank = adapter_down_factor.shape[:2]
    owned = adapters // wa_size
    tiles = token_rows // TILE
    sub_width = group_width // dev_size

    own_adapter = lax.dynamic_slice_in_dim(tile_owner_adapter[:, 0], me * tiles, tiles)
    own_live = lax.dynamic_slice_in_dim(tile_live_count, me * tiles, tiles)
    begin = jnp.cumsum(own_live) - own_live
    position = jnp.arange(token_rows, dtype=jnp.int32) % TILE
    target = jnp.where(
        position < jnp.repeat(own_live, TILE), jnp.repeat(begin, TILE) + position, -1
    )
    pick = (jnp.arange(rows, dtype=jnp.int32)[:, None] == target[None, :]).astype(BF16)
    row_adapter = jnp.repeat(own_adapter, TILE)

    def compact(values):
        return jnp.dot(pick, values, preferred_element_type=F32).astype(BF16)

    pieces = []
    for flip in (1, 0):
        for ahead in range(length):
            target_device = jnp.array(group.table(-ahead, flip), jnp.int32)[me]
            piece = compact(
                lax.dynamic_slice_in_dim(
                    output_gradient, target_device * group_width + dev * sub_width, sub_width, 1
                )
            )
            if flip or ahead:
                piece = lax.ppermute(piece, "wa", group.fetch_pairs(ahead, flip))
            pieces.append(piece)
    mine = jnp.concatenate(pieces, axis=0)
    _, held, spans = butterfly_gather(mine, dev_size)
    place_of = jnp.array([spans.index(j) for j in range(dev_size)], jnp.int32)
    columns = jnp.concatenate(
        [
            lax.dynamic_index_in_dim(held, place_of[jnp.bitwise_xor(dev, j)], 0, keepdims=False)
            for j in range(dev_size)
        ],
        axis=1,
    )
    columns_other = columns[: length * rows]
    columns_own = columns[length * rows :]

    flat_down = adapter_down_factor.reshape(adapters * rank, hidden_local)
    flat_up = adapter_up_factor.reshape(adapters * rank, shard_columns)
    grad_slice = compact(
        lax.dynamic_slice_in_dim(output_gradient, dev * shard_columns, shard_columns, 1)
    )
    gate = compact(gate_preactivation).astype(F32)
    up = compact(up_preactivation).astype(F32)
    hidden = (jax.nn.silu(gate) * up).astype(BF16)

    def selector_for(order):
        return jnp.dot(
            pick, (row_adapter[:, None] == order[None, :]).astype(BF16), preferred_element_type=F32
        )

    adapter_order = jnp.arange(adapters, dtype=jnp.int32)
    selector = selector_for(adapter_order)
    owners = jnp.array(
        [group.table(ahead, flip) for ahead in range(length) for flip in (1, 0)], jnp.int32
    )[:, me]
    owner_order = (owners[:, None] * owned + jnp.arange(owned, dtype=jnp.int32)).reshape(adapters)
    owner_selector = selector_for(owner_order)

    def choose(values):
        return jnp.sum(
            values.reshape(rows, adapters, rank) * selector[:, :, None], axis=1
        )

    def spread(values, which):
        wide = values[:, None, :] * which.astype(BF16)[:, :, None]
        return wide.reshape(rows, adapters * rank)

    lora = jnp.concatenate(
        [choose(nt_dot(hidden, flat_down)), choose(nt_dot(grad_slice, flat_up))], axis=1
    )
    lora = butterfly_sum(lora, dev_size).astype(BF16)
    lora_in, lora_out = lora[:, :rank], lora[:, rank:]
    spread_out = spread(lora_out, selector)

    def owner_sum(lora_values, values):
        partial = tn_dot(spread(lora_values, owner_selector), values).astype(BF16)
        partial = partial.reshape(length, 2, owned * rank, values.shape[1])
        both = ring_sum(group, [partial[k] for k in range(length)])
        arrived = lax.ppermute(both[0].astype(BF16), "wa", group.swap_pairs())
        total = 2.0 * (both[1] + arrived.astype(F32))
        return total.reshape(owned, rank, values.shape[1])

    grad_a = owner_sum(lora_out, hidden)
    grad_b = owner_sum(lora_in, grad_slice)

    chunks = chunk_count(hidden_local)
    width = hidden_local // chunks
    grad_gate_parts, grad_up_parts = [], []
    for chunk in range(chunks):
        span = slice(chunk * width, (chunk + 1) * width)
        weights = down_weight[span]
        away = nt_dot(columns_other, weights).astype(BF16)
        arrived = lax.ppermute(away, "wa", group.swap_pairs())
        paired = add_round(nt_dot(columns_own, weights), arrived)
        base = ring_sum(group, [paired[k * rows : (k + 1) * rows] for k in range(length)])
        hidden_grad = base + 2.0 * jnp.dot(
            spread_out, flat_down[:, span], preferred_element_type=F32
        )
        gate_here, up_here = gate[:, span], up[:, span]
        sigmoid = jax.nn.sigmoid(gate_here)
        grad_up = (hidden_grad * gate_here * sigmoid).astype(BF16)
        grad_gate = (
            hidden_grad * up_here * sigmoid * (1.0 + gate_here * (1.0 - sigmoid))
        ).astype(BF16)
        grad_up_parts.append(tn_dot(pick, grad_up).astype(BF16))
        grad_gate_parts.append(tn_dot(pick, grad_gate).astype(BF16))
    return (
        jnp.concatenate(grad_gate_parts, axis=1),
        jnp.concatenate(grad_up_parts, axis=1),
        grad_a,
        grad_b,
    )


def solution(mesh):
    wa_size, dev_size = mesh.shape["wa"], mesh.shape["dev"]

    def on_device(output_gradient, *others):
        return run(output_gradient.shape[0], wa_size, dev_size, output_gradient, *others)

    placed = (
        P("wa", None),
        P("dev", "wa"),
        P("wa", "dev"),
        P("wa", "dev"),
        P(None, None, "dev"),
        P(None, None, "dev"),
        P(),
        P(),
    )
    return jax.shard_map(
        on_device,
        mesh=mesh,
        in_specs=placed,
        out_specs=(P("wa", "dev"), P("wa", "dev"), P("wa", None, "dev"), P("wa", None, "dev")),
        check_vma=False,
    )
```

```python
import jax
import jax.numpy as jnp
from jax import lax
from jax.sharding import PartitionSpec as P

TILE = 16
BF16 = jnp.bfloat16
F32 = jnp.float32


def nt_dot(left, right):
    return lax.dot_general(left, right, (((1,), (1,)), ((), ())), preferred_element_type=F32)


def tn_dot(left, right):
    return lax.dot_general(left, right, (((0,), (0,)), ((), ())), preferred_element_type=F32)


def nn_dot(left, right):
    return jnp.dot(left, right, preferred_element_type=F32)


def xor_permute(value, axis, size, distance):
    return lax.ppermute(value, axis, [(d, d ^ distance) for d in range(size)])


def ordered_offsets(bits):
    offsets = [0]
    for bit in reversed(bits):
        offsets = [o | bit for o in offsets] + offsets
    return offsets


class Lane:
    def __init__(self, chain, fences):
        self.chain = chain
        self.fences = list(fences)
        self.result = None
        self.value = self.take(next(chain))

    def take(self, step):
        value, axis, size, distance = step
        return xor_permute(value, axis, size, distance) if distance else value

    def advance(self, value):
        try:
            self.value = self.take(self.chain.send(value))
        except StopIteration as end:
            self.result = end.value


class Cell:
    def __init__(self, value):
        self.value = value


class Timeline:
    def __init__(self):
        self.now = -1
        self.lanes = []
        self.cells = []

    def lane(self, chain, fences):
        lane = Lane(chain, fences)
        self.lanes.append(lane)
        return lane

    def prepare(self, value):
        cell = Cell(value)
        self.cells.append(cell)
        return cell

    def fence(self):
        self.now += 1
        due = [lane for lane in self.lanes if lane.fences and lane.fences[0] == self.now]
        cells, self.cells = self.cells, []
        leaves, tree = jax.tree.flatten(
            ([lane.value for lane in due], [cell.value for cell in cells])
        )
        values, prepared = jax.tree.unflatten(tree, lax.optimization_barrier(tuple(leaves)))
        for cell, value in zip(cells, prepared):
            cell.value = value
        for lane, value in zip(due, values):
            lane.fences.pop(0)
            lane.advance(value)

    def idle(self):
        return not self.cells and all(lane.result is not None for lane in self.lanes)


def hold(value):
    return value, None, None, 0


def single(value, size, distance):
    value = yield hold(value)
    arrived = yield value, "wa", size, distance
    return arrived


def gather_dev(block, size, distances):
    held, offsets = block[None], [0]
    for distance in distances:
        arrived = yield held, "dev", size, distance
        held = jnp.concatenate([held, arrived], axis=0)
        offsets = offsets + [o ^ distance for o in offsets]
    return held, offsets


def sum_dev(value, size, distances):
    for distance in distances:
        arrived = yield value, "dev", size, distance
        value = value + arrived
    return value


def scatter_sum(away, kept, size, bits, held_steps=()):
    for index, bit in enumerate(bits):
        if index in held_steps:
            away = yield hold(away)
        arrived = yield away, "wa", size, bit
        total = kept.value.astype(F32) + arrived.astype(F32)
        if index + 1 < len(bits):
            half = total.shape[0] // 2
            total = total.astype(BF16)
            away, kept = total[:half], Cell(total[half:])
    return total


def run(
    rows,
    wa_size,
    dev_size,
    output_gradient,
    down_weight,
    gate_preactivation,
    up_preactivation,
    adapter_down_factor,
    adapter_up_factor,
    tile_owner_adapter,
    tile_live_count,
):
    me = lax.axis_index("wa")
    dev = lax.axis_index("dev")
    token_rows = output_gradient.shape[0]
    hidden_local, group_width = down_weight.shape
    shard_columns = adapter_up_factor.shape[2]
    adapters, rank = adapter_down_factor.shape[:2]
    owned = adapters // wa_size
    tiles = token_rows // TILE
    sub_width = group_width // dev_size
    wa_bits = [1 << b for b in range(wa_size.bit_length() - 1)]
    ring_bits = wa_bits[1:] + wa_bits[:1]
    dev_steps = [1 << b for b in reversed(range(dev_size.bit_length() - 1))]
    offsets = ordered_offsets(wa_bits)
    half = len(offsets) // 2
    time = Timeline()

    all_tiles = jnp.arange(tile_live_count.shape[0], dtype=jnp.int32)[:, None]
    row = jnp.arange(token_rows, dtype=jnp.int32)
    tile_of_row = me * tiles + row // TILE
    here = all_tiles == tile_of_row[None, :]
    before = (all_tiles >= me * tiles) & (all_tiles < tile_of_row[None, :])
    live = jnp.sum(jnp.where(here, tile_live_count[:, None], 0), axis=0)
    begin = jnp.sum(jnp.where(before, tile_live_count[:, None], 0), axis=0)
    row_adapter = jnp.sum(jnp.where(here, tile_owner_adapter, 0), axis=0)
    position = row % TILE
    target = jnp.where(position < live, begin + position, -1)
    pick = (jnp.arange(rows, dtype=jnp.int32)[:, None] == target[None, :]).astype(BF16)

    def compact(values):
        return nn_dot(pick, values).astype(BF16)

    pieces = [
        compact(
            lax.dynamic_slice_in_dim(
                output_gradient,
                jnp.bitwise_xor(me, offset) * group_width + dev * sub_width,
                sub_width,
                1,
            )
        )
        for offset in offsets
    ]
    lanes = [
        time.lane(single(piece, wa_size, offset), [0, 1] if k < half else [1, 2])
        for k, (piece, offset) in enumerate(zip(pieces, offsets))
        if offset
    ]
    gradient = time.prepare(output_gradient)
    time.fence()

    flat_up = adapter_up_factor.reshape(adapters * rank, shard_columns)
    flat_down = adapter_down_factor.reshape(adapters * rank, hidden_local)

    def selector_for(order):
        return nn_dot(pick, (row_adapter[:, None] == order[None, :]).astype(BF16)).astype(BF16)

    selector = selector_for(jnp.arange(adapters, dtype=jnp.int32))

    def choose(values):
        wide = values.reshape(rows, adapters, rank) * selector.astype(F32)[:, :, None]
        return jnp.sum(wide, axis=1)

    def spread(values, which):
        wide = values[:, None, :] * which[:, :, None]
        return wide.reshape(rows, adapters * rank)

    grad_slice = compact(
        lax.dynamic_slice_in_dim(gradient.value, dev * shard_columns, shard_columns, 1)
    )
    out_partial = time.prepare(choose(nt_dot(grad_slice, flat_up)))
    gate_all, up_all = time.prepare(gate_preactivation), time.prepare(up_preactivation)
    time.fence()

    steps = len(dev_steps)
    first = jnp.concatenate([lane.result for lane in lanes[:half]], axis=0)
    first_lane = time.lane(gather_dev(first, dev_size, dev_steps), range(2, 2 + steps))
    out_lane = time.lane(sum_dev(out_partial.value, dev_size, dev_steps), range(2, 2 + steps))
    gate = time.prepare(compact(gate_all.value))
    up = time.prepare(compact(up_all.value))
    hidden = time.prepare(
        (jax.nn.silu(gate.value.astype(F32)) * up.value.astype(F32)).astype(BF16)
    )
    time.fence()

    second = jnp.concatenate([lane.result for lane in lanes[half:]] + [pieces[-1]], axis=0)
    second_lane = time.lane(gather_dev(second, dev_size, dev_steps), range(3, 3 + steps))
    in_partial = time.prepare(choose(nt_dot(hidden.value, flat_down)))
    for _ in range(steps - 1):
        time.fence()

    start = time.now
    in_lane = time.lane(
        sum_dev(in_partial.value, dev_size, dev_steps), range(start + 1, start + 1 + steps)
    )
    lora_out = out_lane.result.astype(BF16)
    spread_out = time.prepare(spread(lora_out, selector))

    def assemble(lane):
        held, spans = lane.result
        place = jnp.array([spans.index(j) for j in range(dev_size)], jnp.int32)
        parts = [
            lax.dynamic_index_in_dim(held, place[jnp.bitwise_xor(dev, j)], 0, keepdims=False)
            for j in range(dev_size)
        ]
        return jnp.concatenate(parts, axis=1)

    def adapter_chain(values, others, bits, held_steps=()):
        owners = jnp.bitwise_xor(me, jnp.array(ordered_offsets(bits), jnp.int32))
        order = owners[:, None] * owned + jnp.arange(owned, dtype=jnp.int32)
        owner_spread = spread(values, selector_for(order.reshape(adapters)))
        partial = tn_dot(owner_spread, others).astype(BF16)
        middle = partial.shape[0] // 2
        return scatter_sum(partial[:middle], Cell(partial[middle:]), wa_size, bits, held_steps)

    units = 14 if hidden_local % (14 * 128) == 0 else 1
    unit = hidden_local // units
    widths = [2, 2, 2, 2, 2, 2, 1, 1] if units == 14 else [1]
    count = len(widths)
    spans = [
        slice(sum(widths[:k]) * unit, sum(widths[: k + 1]) * unit) for k in range(count)
    ]
    depth = len(wa_bits)
    base_lanes, own = {}, {}
    columns_away, columns_own = Cell(assemble(first_lane)), Cell(None)
    renewed = [columns_away, hidden]

    def fence():
        time.cells.extend(renewed)
        time.fence()

    def launch(chunk):
        if chunk >= count:
            return
        away = nt_dot(columns_away.value, down_weight[spans[chunk]]).astype(BF16)
        own[chunk] = Cell(None)
        send = start + chunk
        arrive = start + 2 + chunk
        held = (0,) if send > time.now else ()
        base_lanes[chunk] = time.lane(
            scatter_sum(away, own[chunk], wa_size, wa_bits, held),
            [send] * len(held) + list(range(arrive, arrive + depth)),
        )

    def fill(chunk):
        if chunk < count:
            own[chunk].value = nt_dot(columns_own.value, down_weight[spans[chunk]]).astype(BF16)
            time.cells.append(own[chunk])

    def finish(chunk):
        span = spans[chunk]
        hidden_grad = base_lanes[chunk].result + 2.0 * nn_dot(
            spread_out.value, flat_down[:, span]
        )
        gate_here, up_here = gate.value[:, span].astype(F32), up.value[:, span].astype(F32)
        sigmoid = jax.nn.sigmoid(gate_here)
        grad_up = (hidden_grad * gate_here * sigmoid).astype(BF16)
        grad_gate = (
            hidden_grad * up_here * sigmoid * (1.0 + gate_here * (1.0 - sigmoid))
        ).astype(BF16)
        return time.prepare((tn_dot(pick, grad_gate).astype(BF16), tn_dot(pick, grad_up).astype(BF16)))

    cut = hidden_local // 2
    last = depth - 1
    late = max(start + 8, start + 2 + last)
    launch(0)
    late_lane = time.lane(
        adapter_chain(lora_out, hidden.value[:, cut:], ring_bits, (last,)),
        list(range(start + 2, start + 2 + last)) + [late, late + 1],
    )
    launch(1)
    fence()
    columns_own.value = assemble(second_lane)
    renewed.append(columns_own)
    launch(2)
    fill(0)
    done = {}
    b_lane = early_lane = None
    while not (len(done) == count and b_lane and time.idle()):
        fence()
        now = time.now - start
        for chunk, lane in base_lanes.items():
            if lane.result is not None and chunk not in done:
                done[chunk] = finish(chunk)
        if b_lane is None and in_lane.result is not None:
            final = max(late + 1, time.now + depth)
            b_lane = time.lane(
                adapter_chain(in_lane.result.astype(BF16), grad_slice, ring_bits, (last,)),
                list(range(time.now + 1, time.now + 1 + last)) + [final, final + 1],
            )
        if early_lane is None and now >= 4:
            early_lane = time.lane(
                adapter_chain(lora_out, hidden.value[:, :cut], wa_bits),
                range(time.now + 2, time.now + 2 + depth),
            )
        launch(now + 1)
        fill(now - 1)

    grad_a = 2.0 * jnp.concatenate([early_lane.result, late_lane.result], axis=1)
    grad_b = 2.0 * b_lane.result
    return (
        jnp.concatenate([done[k].value[0] for k in range(count)], axis=1),
        jnp.concatenate([done[k].value[1] for k in range(count)], axis=1),
        grad_a.reshape(owned, rank, hidden_local),
        grad_b.reshape(owned, rank, shard_columns),
    )


def solution(mesh):
    wa_size, dev_size = mesh.shape["wa"], mesh.shape["dev"]

    def on_device(output_gradient, *others):
        return run(output_gradient.shape[0], wa_size, dev_size, output_gradient, *others)

    placed = (
        P("wa", None),
        P("dev", "wa"),
        P("wa", "dev"),
        P("wa", "dev"),
        P(None, None, "dev"),
        P(None, None, "dev"),
        P(),
        P(),
    )
    return jax.shard_map(
        on_device,
        mesh=mesh,
        in_specs=placed,
        out_specs=(P("wa", "dev"), P("wa", "dev"), P("wa", None, "dev"), P("wa", None, "dev")),
        check_vma=False,
    )
```

```python
import functools

import jax
import jax.numpy as jnp
from jax import lax
from jax.sharding import PartitionSpec as P

TILE = 16
BF16 = jnp.bfloat16
F32 = jnp.float32


def nt_dot(left, right):
    return lax.dot_general(left, right, (((1,), (1,)), ((), ())), preferred_element_type=F32)


def tn_dot(left, right):
    return lax.dot_general(left, right, (((0,), (0,)), ((), ())), preferred_element_type=F32)


def nn_dot(left, right):
    return jnp.dot(left, right, preferred_element_type=F32)


def xor_permute(value, axis, size, distance):
    return lax.ppermute(value, axis, [(d, d ^ distance) for d in range(size)])


def ordered_offsets(bits):
    offsets = [0]
    for bit in reversed(bits):
        offsets = [o | bit for o in offsets] + offsets
    return offsets


class Lane:
    def __init__(self, chain, fences):
        self.chain = chain
        self.fences = list(fences)
        self.result = None
        self.value = self.take(next(chain))

    def take(self, step):
        value, axis, size, distance = step
        return xor_permute(value, axis, size, distance) if distance else value

    def advance(self, value):
        try:
            self.value = self.take(self.chain.send(value))
        except StopIteration as end:
            self.result = end.value


class Cell:
    def __init__(self, value):
        self.value = value


class Timeline:
    def __init__(self):
        self.now = -1
        self.lanes = []
        self.cells = []

    def lane(self, chain, fences):
        lane = Lane(chain, fences)
        self.lanes.append(lane)
        return lane

    def prepare(self, value):
        cell = Cell(value)
        self.cells.append(cell)
        return cell

    def fence(self):
        self.now += 1
        due = [lane for lane in self.lanes if lane.fences and lane.fences[0] == self.now]
        cells, self.cells = self.cells, []
        leaves, tree = jax.tree.flatten(
            ([lane.value for lane in due], [cell.value for cell in cells])
        )
        values, prepared = jax.tree.unflatten(tree, lax.optimization_barrier(tuple(leaves)))
        for cell, value in zip(cells, prepared):
            cell.value = value
        for lane, value in zip(due, values):
            lane.fences.pop(0)
            lane.advance(value)

    def idle(self):
        return not self.cells and all(lane.result is not None for lane in self.lanes)


def hold(value):
    return value, None, None, 0


def single(value, size, distance):
    value = yield hold(value)
    arrived = yield value, "wa", size, distance
    return arrived


def gather_dev(block, size, distances):
    held = block[None]
    for distance in distances:
        arrived = yield held, "dev", size, distance
        held = jnp.concatenate([held, arrived], axis=0)
    return held


def sum_dev(value, size, distances):
    for distance in distances:
        arrived = yield value, "dev", size, distance
        value = value + arrived
    return value


def scatter_sum(away, kept, size, bits, held_steps=()):
    for index, bit in enumerate(bits):
        if index in held_steps:
            away = yield hold(away)
        arrived = yield away, "wa", size, bit
        total = kept.value.astype(F32) + arrived.astype(F32)
        if index + 1 < len(bits):
            half = total.shape[0] // 2
            total = total.astype(BF16)
            away, kept = total[:half], Cell(total[half:])
    return total


def run(
    rows,
    wa_size,
    dev_size,
    output_gradient,
    down_weight,
    gate_preactivation,
    up_preactivation,
    adapter_down_factor,
    adapter_up_factor,
    tile_owner_adapter,
    tile_live_count,
):
    me = lax.axis_index("wa")
    dev = lax.axis_index("dev")
    token_rows = output_gradient.shape[0]
    hidden_local, group_width = down_weight.shape
    shard_columns = adapter_up_factor.shape[2]
    adapters, rank = adapter_down_factor.shape[:2]
    owned = adapters // wa_size
    tiles = token_rows // TILE
    sub_width = group_width // dev_size
    wa_bits = [1 << b for b in range(wa_size.bit_length() - 1)]
    ring_bits = wa_bits[1:] + wa_bits[:1]
    dev_steps = [1 << b for b in reversed(range(dev_size.bit_length() - 1))]
    offsets = ordered_offsets(wa_bits)
    half = len(offsets) // 2
    time = Timeline()

    all_tiles = jnp.arange(tile_live_count.shape[0], dtype=jnp.int32)[:, None]
    row = jnp.arange(token_rows, dtype=jnp.int32)
    tile_of_row = me * tiles + row // TILE
    here = all_tiles == tile_of_row[None, :]
    before = (all_tiles >= me * tiles) & (all_tiles < tile_of_row[None, :])
    live = jnp.sum(jnp.where(here, tile_live_count[:, None], 0), axis=0)
    begin = jnp.sum(jnp.where(before, tile_live_count[:, None], 0), axis=0)
    row_adapter = jnp.sum(jnp.where(here, tile_owner_adapter, 0), axis=0)
    position = row % TILE
    target = jnp.where(position < live, begin + position, -1)
    pick = (jnp.arange(rows, dtype=jnp.int32)[:, None] == target[None, :]).astype(BF16)

    def compact(values):
        return nn_dot(pick, values).astype(BF16)

    pieces = [
        compact(
            lax.dynamic_slice_in_dim(
                output_gradient,
                jnp.bitwise_xor(me, offset) * group_width + dev * sub_width,
                sub_width,
                1,
            )
        )
        for offset in offsets
    ]
    lanes = [
        time.lane(single(piece, wa_size, offset), [0, 1] if k < half else [1, 2])
        for k, (piece, offset) in enumerate(zip(pieces, offsets))
        if offset
    ]
    gradient = time.prepare(output_gradient)
    time.fence()

    flat_up = adapter_up_factor.reshape(adapters * rank, shard_columns)
    flat_down = adapter_down_factor.reshape(adapters * rank, hidden_local)

    def selector_for(order):
        return nn_dot(pick, (row_adapter[:, None] == order[None, :]).astype(BF16)).astype(BF16)

    selector = selector_for(jnp.arange(adapters, dtype=jnp.int32))

    def choose(values):
        wide = values.reshape(rows, adapters, rank) * selector.astype(F32)[:, :, None]
        return jnp.sum(wide, axis=1)

    def spread(values, which):
        wide = values[:, None, :] * which[:, :, None]
        return wide.reshape(rows, adapters * rank)

    grad_slice = compact(
        lax.dynamic_slice_in_dim(gradient.value, dev * shard_columns, shard_columns, 1)
    )
    out_partial = time.prepare(choose(nt_dot(grad_slice, flat_up)))
    gate_all, up_all = time.prepare(gate_preactivation), time.prepare(up_preactivation)
    time.fence()

    steps = len(dev_steps)
    first = jnp.concatenate([lane.result for lane in lanes[:half]], axis=0)
    first_lane = time.lane(gather_dev(first, dev_size, dev_steps), range(2, 2 + steps))
    out_lane = time.lane(sum_dev(out_partial.value, dev_size, dev_steps), range(2, 2 + steps))
    gate = time.prepare(compact(gate_all.value))
    up = time.prepare(compact(up_all.value))
    hidden = time.prepare(
        (jax.nn.silu(gate.value.astype(F32)) * up.value.astype(F32)).astype(BF16)
    )
    time.fence()

    second = jnp.concatenate([lane.result for lane in lanes[half:]] + [pieces[-1]], axis=0)
    second_lane = time.lane(
        gather_dev(second, dev_size, dev_steps), range(2 + steps, 2 + 2 * steps)
    )
    in_partial = time.prepare(choose(nt_dot(hidden.value, flat_down)))
    for _ in range(steps - 1):
        time.fence()

    start = time.now
    in_lane = time.lane(
        sum_dev(in_partial.value, dev_size, dev_steps), range(start + 1, start + 1 + steps)
    )
    lora_out = out_lane.result.astype(BF16)
    spread_out = time.prepare(spread(lora_out, selector))

    def place_of(offset):
        bits = [((offset // step) % 2) * (dev_size // (2 * step)) for step in dev_steps]
        return sum(bits)

    def assemble(lane):
        held = lane.result
        parts = [
            lax.dynamic_index_in_dim(held, place_of(jnp.bitwise_xor(dev, j)), 0, keepdims=False)
            for j in range(dev_size)
        ]
        return jnp.concatenate(parts, axis=1)

    def adapter_chain(values, others, bits, held_steps=()):
        owners = jnp.bitwise_xor(me, jnp.array(ordered_offsets(bits), jnp.int32))
        order = owners[:, None] * owned + jnp.arange(owned, dtype=jnp.int32)
        owner_spread = spread(values, selector_for(order.reshape(adapters)))
        partial = tn_dot(owner_spread, others).astype(BF16)
        middle = partial.shape[0] // 2
        return scatter_sum(partial[:middle], Cell(partial[middle:]), wa_size, bits, held_steps)

    widths = [2, 2, 2, 2, 2, 2, 1, 1]
    unit = hidden_local // sum(widths)
    count = len(widths)
    spans = [
        slice(sum(widths[:k]) * unit, sum(widths[: k + 1]) * unit) for k in range(count)
    ]
    depth = len(wa_bits)
    origin = start + steps + 1
    base_lanes, own = {}, {}
    columns_away, columns_own = Cell(assemble(first_lane)), Cell(None)
    renewed = [columns_away, hidden]

    def fence():
        time.cells.extend(renewed)
        time.fence()

    def launch(chunk):
        if chunk >= count or chunk in base_lanes:
            return
        away = nt_dot(columns_away.value, down_weight[spans[chunk]]).astype(BF16)
        own[chunk] = Cell(None)
        arrive = origin + 2 * chunk
        send = arrive - 4
        held = (0,) if send > time.now else ()
        more = [arrive + 2 * k - 1 for k in range(1, depth)]
        if chunk == count - 1:
            more = [arrive + k for k in range(1, depth)]
        base_lanes[chunk] = time.lane(
            scatter_sum(away, own[chunk], wa_size, wa_bits, held),
            [send] * len(held) + [arrive] + more,
        )

    def fill(chunk):
        if 0 <= chunk < count:
            own[chunk].value = nt_dot(columns_own.value, down_weight[spans[chunk]]).astype(BF16)
            time.cells.append(own[chunk])

    def finish(chunk):
        span = spans[chunk]
        hidden_grad = base_lanes[chunk].result + 2.0 * nn_dot(
            spread_out.value, flat_down[:, span]
        )
        gate_here, up_here = gate.value[:, span].astype(F32), up.value[:, span].astype(F32)
        sigmoid = jax.nn.sigmoid(gate_here)
        grad_up = (hidden_grad * gate_here * sigmoid).astype(BF16)
        grad_gate = (
            hidden_grad * up_here * sigmoid * (1.0 + gate_here * (1.0 - sigmoid))
        ).astype(BF16)
        return time.prepare((tn_dot(pick, grad_gate).astype(BF16), tn_dot(pick, grad_up).astype(BF16)))

    seventh = hidden_local // 7
    parts_a = [slice(0, 2 * seventh), slice(2 * seventh, 4 * seventh), slice(4 * seventh, None)]
    last = depth - 1
    late = max(origin + 10, origin + 2 * last + 1)
    launch(0)
    late_lane = time.lane(
        adapter_chain(lora_out, hidden.value[:, parts_a[2]], ring_bits, (last,)),
        [origin + 2 * k for k in range(last)] + [late, late + 2],
    )
    launch(1)
    b_lane = None
    early_lanes = []
    done = {}
    while not (len(done) == count and b_lane and time.idle()):
        fence()
        now = time.now - origin
        for chunk, lane in base_lanes.items():
            if lane.result is not None and chunk not in done:
                done[chunk] = finish(chunk)
        if columns_own.value is None and second_lane.result is not None:
            columns_own.value = assemble(second_lane)
            renewed.append(columns_own)
        if now % 2:
            fill((now + 1) // 2)
            launch((now + 1) // 2 + 2)
        if b_lane is None and in_lane.result is not None:
            b_lane = time.lane(
                adapter_chain(in_lane.result.astype(BF16), grad_slice, ring_bits, (last,)),
                [origin + 2 * k + 3 for k in range(last)] + [late + 1, late + 3],
            )
        if now in (2, 6):
            part = parts_a[len(early_lanes)]
            early_lanes.append(
                time.lane(
                    adapter_chain(lora_out, hidden.value[:, part], wa_bits),
                    [time.now + 3 + 2 * k for k in range(depth)],
                )
            )

    grad_a = 2.0 * jnp.concatenate(
        [lane.result for lane in early_lanes] + [late_lane.result], axis=1
    )
    grad_b = 2.0 * b_lane.result
    return (
        jnp.concatenate([done[k].value[0] for k in range(count)], axis=1),
        jnp.concatenate([done[k].value[1] for k in range(count)], axis=1),
        grad_a.reshape(owned, rank, hidden_local),
        grad_b.reshape(owned, rank, shard_columns),
    )


def solution(mesh):
    wa_size, dev_size = mesh.shape["wa"], mesh.shape["dev"]

    def on_device(output_gradient, *others):
        live = others[-1].reshape(wa_size, -1)
        most = jnp.max(jnp.sum(live, axis=1))
        token_rows = output_gradient.shape[0]
        sizes = [token_rows * part // 16 for part in (10, 11, 12, 13, 16)]
        branch = sum((most > size).astype(jnp.int32) for size in sizes[:-1])
        programs = [functools.partial(run, size, wa_size, dev_size) for size in sizes]
        return lax.switch(branch, programs, output_gradient, *others)

    placed = (
        P("wa", None),
        P("dev", "wa"),
        P("wa", "dev"),
        P("wa", "dev"),
        P(None, None, "dev"),
        P(None, None, "dev"),
        P(),
        P(),
    )
    return jax.shard_map(
        on_device,
        mesh=mesh,
        in_specs=placed,
        out_specs=(P("wa", "dev"), P("wa", "dev"), P("wa", None, "dev"), P("wa", None, "dev")),
        check_vma=False,
    )
```

```python
import functools

import jax
import jax.numpy as jnp
from jax import lax
from jax.sharding import PartitionSpec as P

TILE = 16
BF16 = jnp.bfloat16
F32 = jnp.float32

PLAN = (
    ("a0", "y", 7),
    ("a1", "z", 7),
    ("b0", "y", 2),
    ("b1", "y", 2),
    ("b2", "x", 1),
    ("b3", "y", 3),
    ("b4", "y", 2),
    ("b5", "y", 2),
    ("b6", "y", 1),
    ("b7", "y", 1),
    ("g", "x", 0),
)
EVENTS = (
    "b1", "a0", "a1", "b4", "b3", "b1", "a0", "a1", "b4", "a0",
    "b2", "b1", "b4", "b1", "b5", "b3", "b4", "b2", "a1", "g",
    "b3", "b0", "b5", "b2", "b3", "b6", "b2", "g", "b0", "b5",
    "b7", "b6", "g", "b5", "b0", "b7", "g", "b6", "b0", "b7",
    "b6", "b7",
)


def nt_dot(left, right):
    return lax.dot_general(left, right, (((1,), (1,)), ((), ())), preferred_element_type=F32)


def tn_dot(left, right):
    return lax.dot_general(left, right, (((0,), (0,)), ((), ())), preferred_element_type=F32)


def nn_dot(left, right):
    return jnp.dot(left, right, preferred_element_type=F32)


def xor_permute(value, axis, size, distance):
    return lax.ppermute(value, axis, [(d, d ^ distance) for d in range(size)])


def ordered_offsets(bits):
    offsets = [0]
    for bit in reversed(bits):
        offsets = [o | bit for o in offsets] + offsets
    return offsets


class Lane:
    def __init__(self, chain):
        self.chain = chain
        self.result = None
        self.value = xor_permute(*next(chain))

    def advance(self, value):
        try:
            self.value = xor_permute(*self.chain.send(value))
        except StopIteration as end:
            self.result = end.value


class Cell:
    def __init__(self, value):
        self.value = value


class Timeline:
    def __init__(self):
        self.cells = []
        self.renewed = []

    def prepare(self, value):
        cell = Cell(value)
        self.cells.append(cell)
        return cell

    def fence(self, *lanes):
        cells, self.cells = self.cells + self.renewed, []
        leaves, tree = jax.tree.flatten(
            ([lane.value for lane in lanes], [cell.value for cell in cells])
        )
        values, prepared = jax.tree.unflatten(tree, lax.optimization_barrier(tuple(leaves)))
        for cell, value in zip(cells, prepared):
            cell.value = value
        for lane, value in zip(lanes, values):
            lane.advance(value)


def single(value, size, distance):
    arrived = yield value, "wa", size, distance
    return arrived


def gather_dev(block, size, distances):
    held = block[None]
    for distance in distances:
        arrived = yield held, "dev", size, distance
        held = jnp.concatenate([held, arrived], axis=0)
    return held


def sum_dev(value, size, distances):
    for distance in distances:
        arrived = yield value, "dev", size, distance
        value = value + arrived
    return value


def scatter_sum(away, kept, size, bits):
    for index, bit in enumerate(bits):
        arrived = yield away, "wa", size, bit
        total = kept.value.astype(F32) + arrived.astype(F32)
        if index + 1 < len(bits):
            half = total.shape[0] // 2
            total = total.astype(BF16)
            away, kept = total[:half], Cell(total[half:])
    return total


def run(
    rows,
    wa_size,
    dev_size,
    output_gradient,
    down_weight,
    gate_preactivation,
    up_preactivation,
    adapter_down_factor,
    adapter_up_factor,
    tile_owner_adapter,
    tile_live_count,
):
    me = lax.axis_index("wa")
    dev = lax.axis_index("dev")
    token_rows = output_gradient.shape[0]
    hidden_local, group_width = down_weight.shape
    shard_columns = adapter_up_factor.shape[2]
    adapters, rank = adapter_down_factor.shape[:2]
    owned = adapters // wa_size
    tiles = token_rows // TILE
    sub_width = group_width // dev_size
    wa_bits = [1 << b for b in range(wa_size.bit_length() - 1)]
    dev_steps = [1 << b for b in reversed(range(dev_size.bit_length() - 1))]
    offsets = ordered_offsets(wa_bits)
    half = len(offsets) // 2
    time = Timeline()

    all_tiles = jnp.arange(tile_live_count.shape[0], dtype=jnp.int32)[:, None]
    row = jnp.arange(token_rows, dtype=jnp.int32)
    tile_of_row = me * tiles + row // TILE
    here = all_tiles == tile_of_row[None, :]
    before = (all_tiles >= me * tiles) & (all_tiles < tile_of_row[None, :])
    live = jnp.sum(jnp.where(here, tile_live_count[:, None], 0), axis=0)
    begin = jnp.sum(jnp.where(before, tile_live_count[:, None], 0), axis=0)
    row_adapter = jnp.sum(jnp.where(here, tile_owner_adapter, 0), axis=0)
    position = row % TILE
    target = jnp.where(position < live, begin + position, -1)
    pick = (jnp.arange(rows, dtype=jnp.int32)[:, None] == target[None, :]).astype(BF16)

    def compact(values):
        return nn_dot(pick, values).astype(BF16)

    gradient = time.prepare(compact(output_gradient))
    gate_all, up_all = time.prepare(gate_preactivation), time.prepare(up_preactivation)
    time.fence()

    def piece(offset):
        begin = jnp.bitwise_xor(me, offset) * group_width + dev * sub_width
        return lax.dynamic_slice_in_dim(gradient.value, begin, sub_width, 1)

    first_pieces = [Lane(single(piece(o), wa_size, o)) for o in offsets[:half]]
    flat_up = adapter_up_factor.reshape(adapters * rank, shard_columns)
    flat_down = adapter_down_factor.reshape(adapters * rank, hidden_local)

    def selector_for(order):
        return nn_dot(pick, (row_adapter[:, None] == order[None, :]).astype(BF16)).astype(BF16)

    selector = selector_for(jnp.arange(adapters, dtype=jnp.int32))

    def choose(values):
        wide = values.reshape(rows, adapters, rank) * selector.astype(F32)[:, :, None]
        return jnp.sum(wide, axis=1)

    def spread(values, which):
        wide = values[:, None, :] * which[:, :, None]
        return wide.reshape(rows, adapters * rank)

    def owner_spread(values, bits):
        place = jnp.arange(adapters, dtype=jnp.int32) // owned
        offset = sum(
            jnp.where((place >> (len(bits) - 1 - k)) & 1 == 0, bit, 0)
            for k, bit in enumerate(bits)
        )
        order = jnp.bitwise_xor(me, offset) * owned + jnp.arange(adapters, dtype=jnp.int32) % owned
        return spread(values, selector_for(order))

    steps = len(dev_steps)
    grad_slice = lax.dynamic_slice_in_dim(gradient.value, dev * shard_columns, shard_columns, 1)
    out_lane = Lane(sum_dev(choose(nt_dot(grad_slice, flat_up)), dev_size, dev_steps))
    gate = time.prepare(compact(gate_all.value))
    up = time.prepare(compact(up_all.value))
    hidden = time.prepare(
        (jax.nn.silu(gate.value.astype(F32)) * up.value.astype(F32)).astype(BF16)
    )
    for _ in range(steps):
        time.fence(out_lane)
    lora_out = out_lane.result.astype(BF16)
    spread_out = spread(lora_out, selector)

    orders = {
        "y": wa_bits,
        "z": wa_bits[1:] + wa_bits[:1],
        "x": [wa_bits[1], wa_bits[0]] + wa_bits[2:],
    }
    unit = hidden_local // 14
    kinds, spans, at = {}, {}, {"a": 0, "b": 0}
    for name, kind, width in PLAN:
        kinds[name] = orders[kind]
        begin = at.get(name[0], 0)
        spans[name] = slice(begin * unit, (begin + width) * unit)
        at[name[0]] = begin + width
    ready, lanes = {}, {}

    def ready_adapter(name, values, others):
        partial = tn_dot(owner_spread(values, kinds[name]), others).astype(BF16)
        middle = partial.shape[0] // 2
        ready[name] = time.prepare(partial[:middle]), time.prepare(partial[middle:])

    def launch(name):
        away, own = ready[name]
        lanes[name] = Lane(scatter_sum(away.value, own, wa_size, kinds[name]))

    ready_adapter("a1", lora_out, hidden.value[:, spans["a1"]])
    time.fence(*first_pieces)
    first = jnp.concatenate([lane.result for lane in first_pieces], axis=0)
    first_lane = Lane(gather_dev(first, dev_size, dev_steps))
    second_pieces = [Lane(single(piece(o), wa_size, o)) for o in offsets[half:-1]]
    launch("a1")
    ready_adapter("a0", lora_out, hidden.value[:, spans["a0"]])
    time.fence(*second_pieces)
    second = jnp.concatenate([lane.result for lane in second_pieces] + [piece(0)], axis=0)
    second_lane = Lane(gather_dev(second, dev_size, dev_steps))
    launch("a0")
    in_partial = time.prepare(choose(nt_dot(hidden.value, flat_down)))
    time.fence(first_lane)
    in_lane = Lane(sum_dev(in_partial.value, dev_size, dev_steps))
    time.fence(second_lane)
    time.fence(in_lane)
    for _ in range(steps - 1):
        time.fence(first_lane)
        time.fence(second_lane)
        time.fence(in_lane)

    def place_of(offset):
        bits = [
            ((offset >> (step.bit_length() - 1)) & 1) * (dev_size // (2 * step))
            for step in dev_steps
        ]
        return sum(bits)

    def assemble(lane):
        held = lane.result
        parts = [
            lax.dynamic_index_in_dim(held, place_of(jnp.bitwise_xor(dev, j)), 0, keepdims=False)
            for j in range(dev_size)
        ]
        return jnp.concatenate(parts, axis=1)

    columns_away, columns_own = Cell(assemble(first_lane)), Cell(assemble(second_lane))
    lora_in = in_lane.result.astype(BF16)
    time.renewed = [columns_away, columns_own, hidden]

    def columns_for(bits):
        if bits == wa_bits:
            return columns_away.value, columns_own.value
        blocks = {}
        for k, offset in enumerate(offsets):
            part = columns_away.value if k < half else columns_own.value
            blocks[offset] = part[(k % half) * rows : (k % half + 1) * rows]
        order = [blocks[offset] for offset in ordered_offsets(bits)]
        return jnp.concatenate(order[:half], axis=0), jnp.concatenate(order[half:], axis=0)

    def make_ready(name):
        if name in ready:
            return
        if name == "g":
            ready_adapter(name, lora_in, grad_slice)
            return
        if name[0] == "a":
            ready_adapter(name, lora_out, hidden.value[:, spans[name]])
            return
        weights = down_weight[spans[name]]
        ready[name] = tuple(
            time.prepare(nt_dot(part, weights).astype(BF16)) for part in columns_for(kinds[name])
        )

    def finish(name):
        span = spans[name]
        hidden_grad = lanes[name].result + 2.0 * nn_dot(spread_out, flat_down[:, span])
        gate_here, up_here = gate.value[:, span].astype(F32), up.value[:, span].astype(F32)
        sigmoid = jax.nn.sigmoid(gate_here)
        grad_up = (hidden_grad * gate_here * sigmoid).astype(BF16)
        grad_gate = (
            hidden_grad * up_here * sigmoid * (1.0 + gate_here * (1.0 - sigmoid))
        ).astype(BF16)
        return time.prepare(
            (tn_dot(pick, grad_gate).astype(BF16), tn_dot(pick, grad_up).astype(BF16))
        )

    done = {}
    for index, name in enumerate(EVENTS):
        for soon in EVENTS[index : index + 3]:
            make_ready(soon)
        if name not in lanes:
            time.fence()
            launch(name)
            continue
        lane = lanes[name]
        time.fence(lane)
        while lane.result is None and name not in EVENTS[index + 1 :]:
            time.fence(lane)
        if lane.result is not None:
            done[name] = finish(name) if name[0] == "b" else Cell(2.0 * lane.result)

    def joined(letter, index=None):
        names = sorted(name for name in done if name[0] == letter)
        values = [done[name].value for name in names]
        return jnp.concatenate(values if index is None else [v[index] for v in values], axis=1)

    return (
        joined("b", 0),
        joined("b", 1),
        joined("a").reshape(owned, rank, hidden_local),
        joined("g").reshape(owned, rank, shard_columns),
    )


def solution(mesh):
    wa_size, dev_size = mesh.shape["wa"], mesh.shape["dev"]

    def on_device(output_gradient, *others):
        token_rows = output_gradient.shape[0]
        live = others[-1]
        tiles = live.shape[0] // wa_size
        shard = jnp.arange(wa_size, dtype=jnp.int32)[None, :]
        tile = jnp.arange(live.shape[0], dtype=jnp.int32)[:, None]
        totals = jnp.sum(jnp.where(tile // tiles == shard, live[:, None], 0), axis=0)
        sizes = [token_rows * part // 16 for part in (10, 11, 12, 13, 16)]
        limits = token_rows * (10 + jnp.arange(len(sizes) - 1, dtype=jnp.int32)) // 16
        above = jnp.max((totals[:, None] > limits[None, :]).astype(jnp.int32), axis=0)
        branch = jnp.sum(above)
        programs = [functools.partial(run, size, wa_size, dev_size) for size in sizes]
        return lax.switch(branch, programs, output_gradient, *others)

    placed = (
        P("wa", None),
        P("dev", "wa"),
        P("wa", "dev"),
        P("wa", "dev"),
        P(None, None, "dev"),
        P(None, None, "dev"),
        P(),
        P(),
    )
    return jax.shard_map(
        on_device,
        mesh=mesh,
        in_specs=placed,
        out_specs=(P("wa", "dev"), P("wa", "dev"), P("wa", None, "dev"), P("wa", None, "dev")),
        check_vma=False,
    )
```

```python
import functools

import jax
import jax.numpy as jnp
from jax import lax
from jax.sharding import PartitionSpec as P

TILE = 16
BF16 = jnp.bfloat16
F32 = jnp.float32

PLAN = (
    ("a0", "y", 2),
    ("a1", "z", 2),
    ("a2", "y", 2),
    ("a3", "y", 5),
    ("a4", "z", 3),
    ("b0", "y", 2),
    ("b1", "y", 2),
    ("b2", "y", 2),
    ("b3", "y", 2),
    ("b4", "y", 2),
    ("b5", "y", 2),
    ("b6", "y", 1),
    ("b7", "y", 1),
    ("g", "z", 0),
)
EVENTS = (
    *("b0", "a0", "a1-", "a3", "a4", "a0", "a2"),
    *("b0", "b1", "a2", "b0", "a4", "a3", "b2", "b0", "a4-"),
    *("b1", "b3", "a3", "g", "b1"),
    *("a3", "b1", "b2", "b4", "g", "b2", "a1"),
    *("b3", "b2", "b5", "g-", "b3"),
    *("b4", "a1", "b3", "b6", "g", "a4", "b4"),
    *("b5", "b4", "b7", "b5"),
    *("b6", "g", "a4", "b7", "b5", "b6", "b7", "b6", "b7"),
)


def nt_dot(left, right):
    return lax.dot_general(left, right, (((1,), (1,)), ((), ())), preferred_element_type=F32)


def tn_dot(left, right):
    return lax.dot_general(left, right, (((0,), (0,)), ((), ())), preferred_element_type=F32)


def nn_dot(left, right):
    return jnp.dot(left, right, preferred_element_type=F32)


def xor_permute(value, axis, size, distance):
    return lax.ppermute(value, axis, [(d, d ^ distance) for d in range(size)])


def ordered_offsets(bits):
    offsets = [0]
    for bit in reversed(bits):
        offsets = [o | bit for o in offsets] + offsets
    return offsets


class Lane:
    def __init__(self, chain):
        self.chain = chain
        self.result = None
        self.request = next(chain)
        self.send(self.request[0])

    def send(self, value):
        self.value = xor_permute(value, *self.request[1:])
        self.request = None

    def advance(self, value, hold):
        if self.request is not None:
            self.send(value)
            return
        try:
            self.request = self.chain.send(value)
            self.value = self.request[0]
            if not hold:
                self.send(self.value)
        except StopIteration as end:
            self.result = end.value


class Cell:
    def __init__(self, value):
        self.value = value


class Timeline:
    def __init__(self):
        self.cells = []
        self.renewed = []

    def prepare(self, value):
        cell = Cell(value)
        self.cells.append(cell)
        return cell

    def fence(self, *lanes, hold=False):
        cells, self.cells = self.cells + self.renewed, []
        leaves, tree = jax.tree.flatten(
            ([lane.value for lane in lanes], [cell.value for cell in cells])
        )
        values, prepared = jax.tree.unflatten(tree, lax.optimization_barrier(tuple(leaves)))
        for cell, value in zip(cells, prepared):
            cell.value = value
        for lane, value in zip(lanes, values):
            lane.advance(value, hold)


def single(value, size, distance):
    arrived = yield value, "wa", size, distance
    return arrived


def gather_dev(block, size, distances):
    held = block[None]
    for distance in distances:
        arrived = yield held, "dev", size, distance
        held = jnp.concatenate([held, arrived], axis=0)
    return held


def sum_dev(value, size, distances):
    for distance in distances:
        arrived = yield value, "dev", size, distance
        value = value + arrived
    return value


def scatter_sum(away, kept, size, bits):
    for index, bit in enumerate(bits):
        arrived = yield away, "wa", size, bit
        total = kept.value.astype(F32) + arrived.astype(F32)
        if index + 1 < len(bits):
            half = total.shape[0] // 2
            total = total.astype(BF16)
            away, kept = total[:half], Cell(total[half:])
    return total


def run(
    rows,
    wa_size,
    dev_size,
    output_gradient,
    down_weight,
    gate_preactivation,
    up_preactivation,
    adapter_down_factor,
    adapter_up_factor,
    tile_owner_adapter,
    tile_live_count,
):
    me = lax.axis_index("wa")
    dev = lax.axis_index("dev")
    token_rows = output_gradient.shape[0]
    hidden_local, group_width = down_weight.shape
    shard_columns = adapter_up_factor.shape[2]
    adapters, rank = adapter_down_factor.shape[:2]
    owned = adapters // wa_size
    tiles = token_rows // TILE
    sub_width = group_width // dev_size
    wa_bits = [1 << b for b in range(wa_size.bit_length() - 1)]
    dev_steps = [1 << b for b in reversed(range(dev_size.bit_length() - 1))]
    offsets = ordered_offsets(wa_bits)
    half = len(offsets) // 2
    time = Timeline()

    all_tiles = jnp.arange(tile_live_count.shape[0], dtype=jnp.int32)[:, None]
    row = jnp.arange(token_rows, dtype=jnp.int32)
    tile_of_row = me * tiles + row // TILE
    here = all_tiles == tile_of_row[None, :]
    before = (all_tiles >= me * tiles) & (all_tiles < tile_of_row[None, :])
    live = jnp.sum(jnp.where(here, tile_live_count[:, None], 0), axis=0)
    begin = jnp.sum(jnp.where(before, tile_live_count[:, None], 0), axis=0)
    row_adapter = jnp.sum(jnp.where(here, tile_owner_adapter, 0), axis=0)
    position = row % TILE
    target = jnp.where(position < live, begin + position, -1)
    pick = (jnp.arange(rows, dtype=jnp.int32)[:, None] == target[None, :]).astype(BF16)

    def compact(values):
        return nn_dot(pick, values).astype(BF16)

    flat_up = adapter_up_factor.reshape(adapters * rank, shard_columns)
    flat_down = adapter_down_factor.reshape(adapters * rank, hidden_local)

    def selector_for(order):
        return nn_dot(pick, (row_adapter[:, None] == order[None, :]).astype(BF16)).astype(BF16)

    selector = selector_for(jnp.arange(adapters, dtype=jnp.int32))

    def choose(values):
        wide = values.reshape(rows, adapters, rank) * selector.astype(F32)[:, :, None]
        return jnp.sum(wide, axis=1)

    def spread(values, which):
        wide = values[:, None, :] * which[:, :, None]
        return wide.reshape(rows, adapters * rank)

    def owner_spread(values, bits):
        place = jnp.arange(adapters, dtype=jnp.int32) // owned
        offset = sum(
            jnp.where((place >> (len(bits) - 1 - k)) & 1 == 0, bit, 0)
            for k, bit in enumerate(bits)
        )
        order = jnp.bitwise_xor(me, offset) * owned + jnp.arange(adapters, dtype=jnp.int32) % owned
        return spread(values, selector_for(order))

    steps = len(dev_steps)
    grad_slice = compact(
        lax.dynamic_slice_in_dim(output_gradient, dev * shard_columns, shard_columns, 1)
    )
    out_partial = time.prepare(choose(nt_dot(grad_slice, flat_up)))
    gradient = time.prepare(output_gradient)
    gate_all, up_all = time.prepare(gate_preactivation), time.prepare(up_preactivation)
    time.fence()
    out_lane = Lane(sum_dev(out_partial.value, dev_size, dev_steps))

    begins = [jnp.bitwise_xor(me, o) * group_width + dev * sub_width for o in offsets]
    mine = jnp.concatenate(
        [lax.dynamic_slice_in_dim(gradient.value, begin, sub_width, 1) for begin in begins], axis=1
    )
    mine = time.prepare(compact(mine))
    time.fence(out_lane)

    def piece(place):
        return mine.value[:, place * sub_width : (place + 1) * sub_width]

    first_pieces = [Lane(single(piece(k), wa_size, offsets[k])) for k in range(half)]
    gate = time.prepare(compact(gate_all.value))
    up = time.prepare(compact(up_all.value))
    hidden = time.prepare(
        (jax.nn.silu(gate.value.astype(F32)) * up.value.astype(F32)).astype(BF16)
    )
    for _ in range(steps - 1):
        time.fence(out_lane)
    lora_out = out_lane.result.astype(BF16)
    spread_out = time.prepare(spread(lora_out, selector))

    orders = {
        "y": wa_bits,
        "z": wa_bits[1:] + wa_bits[:1],
    }
    unit = hidden_local // 14
    kinds, spans, at = {}, {}, {"a": 0, "b": 0}
    for name, kind, width in PLAN:
        kinds[name] = orders[kind]
        begin = at.get(name[0], 0)
        spans[name] = slice(begin * unit, (begin + width) * unit)
        at[name[0]] = begin + width
    ready, lanes = {}, {}

    def ready_adapter(name, values, others):
        partial = tn_dot(owner_spread(values, kinds[name]), others).astype(BF16)
        middle = partial.shape[0] // 2
        ready[name] = time.prepare(partial[:middle]), time.prepare(partial[middle:])

    def launch(name):
        away, own = ready[name]
        lanes[name] = Lane(scatter_sum(away.value, own, wa_size, kinds[name]))

    ready_adapter("a0", lora_out, hidden.value[:, spans["a0"]])
    ready_adapter("a1", lora_out, hidden.value[:, spans["a1"]])
    second_pieces = [
        Lane(single(piece(k), wa_size, offsets[k])) for k in range(half, len(offsets) - 1)
    ]
    time.fence(*first_pieces, *second_pieces)
    first = jnp.concatenate([lane.result for lane in first_pieces], axis=0)
    second = jnp.concatenate(
        [lane.result for lane in second_pieces] + [piece(len(offsets) - 1)], axis=0
    )
    launch("a0")
    launch("a1")
    first_lane = Lane(gather_dev(first, dev_size, dev_steps))
    second_lane = Lane(gather_dev(second, dev_size, dev_steps))
    ready_adapter("a2", lora_out, hidden.value[:, spans["a2"]])
    in_partial = time.prepare(choose(nt_dot(hidden.value, flat_down)))
    time.renewed = [hidden, spread_out]
    time.fence(first_lane, second_lane, lanes["a0"], lanes["a1"])
    launch("a2")
    for _ in range(steps - 2):
        time.fence(first_lane, second_lane)
    time.fence(first_lane, second_lane, lanes["a2"])
    in_lane = Lane(sum_dev(in_partial.value, dev_size, dev_steps))

    def place_of(offset):
        bits = [
            ((offset >> (step.bit_length() - 1)) & 1) * (dev_size // (2 * step))
            for step in dev_steps
        ]
        return sum(bits)

    def assemble(lane):
        held = lane.result
        parts = [
            lax.dynamic_index_in_dim(held, place_of(jnp.bitwise_xor(dev, j)), 0, keepdims=False)
            for j in range(dev_size)
        ]
        return jnp.concatenate(parts, axis=1)

    columns_away, columns_own = Cell(assemble(first_lane)), Cell(assemble(second_lane))
    time.renewed += [columns_away, columns_own]

    def make_ready(name):
        if name in ready:
            return
        if name == "g":
            ready_adapter(name, in_lane.result.astype(BF16), grad_slice)
            return
        if name[0] == "a":
            ready_adapter(name, lora_out, hidden.value[:, spans[name]])
            return
        weights = down_weight[spans[name]]
        ready[name] = tuple(
            time.prepare(nt_dot(part.value, weights).astype(BF16))
            for part in (columns_away, columns_own)
        )

    def finish(name):
        span = spans[name]
        hidden_grad = lanes[name].result + 2.0 * nn_dot(spread_out.value, flat_down[:, span])
        gate_here, up_here = gate.value[:, span].astype(F32), up.value[:, span].astype(F32)
        sigmoid = jax.nn.sigmoid(gate_here)
        grad_up = (hidden_grad * gate_here * sigmoid).astype(BF16)
        grad_gate = (
            hidden_grad * up_here * sigmoid * (1.0 + gate_here * (1.0 - sigmoid))
        ).astype(BF16)
        return time.prepare(
            (tn_dot(pick, grad_gate).astype(BF16), tn_dot(pick, grad_up).astype(BF16))
        )

    done = {}
    names = [event[:2].rstrip("-") for event in EVENTS]
    for index, name in enumerate(names):
        for soon in names[index : index + 3]:
            make_ready(soon)
        if name not in lanes:
            time.fence()
            launch(name)
            while index == 0 and in_lane.result is None:
                time.fence(in_lane)
            continue
        lane = lanes[name]
        time.fence(lane, hold=EVENTS[index].endswith("-"))
        while lane.result is None and name not in names[index + 1 :]:
            time.fence(lane)
        if lane.result is not None:
            done[name] = finish(name) if name[0] == "b" else Cell(2.0 * lane.result)

    def joined(letter, index=None):
        names = sorted(name for name in done if name[0] == letter)
        values = [done[name].value for name in names]
        return jnp.concatenate(values if index is None else [v[index] for v in values], axis=1)

    return (
        joined("b", 0),
        joined("b", 1),
        joined("a").reshape(owned, rank, hidden_local),
        joined("g").reshape(owned, rank, shard_columns),
    )


def solution(mesh):
    wa_size, dev_size = mesh.shape["wa"], mesh.shape["dev"]

    def on_device(output_gradient, *others):
        token_rows = output_gradient.shape[0]
        live = others[-1]
        tiles = live.shape[0] // wa_size
        shard = jnp.arange(wa_size, dtype=jnp.int32)[None, :]
        tile = jnp.arange(live.shape[0], dtype=jnp.int32)[:, None]
        totals = jnp.sum(jnp.where(tile // tiles == shard, live[:, None], 0), axis=0)
        sizes = [token_rows * part // 16 for part in (10, 11, 12, 13, 16)]
        limits = token_rows * (10 + jnp.arange(len(sizes) - 1, dtype=jnp.int32)) // 16
        above = jnp.max((totals[:, None] > limits[None, :]).astype(jnp.int32), axis=0)
        branch = jnp.sum(above)
        programs = [functools.partial(run, size, wa_size, dev_size) for size in sizes]
        return lax.switch(branch, programs, output_gradient, *others)

    placed = (
        P("wa", None),
        P("dev", "wa"),
        P("wa", "dev"),
        P("wa", "dev"),
        P(None, None, "dev"),
        P(None, None, "dev"),
        P(),
        P(),
    )
    return jax.shard_map(
        on_device,
        mesh=mesh,
        in_specs=placed,
        out_specs=(P("wa", "dev"), P("wa", "dev"), P("wa", None, "dev"), P("wa", None, "dev")),
        check_vma=False,
    )
```

```python
import jax
import jax.numpy as jnp
from jax import lax
from jax.sharding import PartitionSpec as P

TILE = 16
BF16 = jnp.bfloat16
F32 = jnp.float32

ROWS = 13

PLAN = (
    ("a0", "y", 2),
    ("a1", "z", 3),
    ("a2", "y", 3),
    ("a3", "y", 4),
    ("a4", "z", 2),
    ("b0", "y", 2),
    ("b1", "y", 2),
    ("b2", "y", 2),
    ("b3", "y", 2),
    ("b4", "y", 2),
    ("b5", "y", 2),
    ("b6", "y", 1),
    ("b7", "z", 1),
    ("g", "z", 0),
)
EVENTS = (
    *("b0", "a0", "a1-", "g", "a3", "a0", "a2", "a4"),
    *("b0", "a2", "b1", "g-", "b0", "a3", "b2", "a4-", "b0"),
    *("b1", "b3", "a3", "g", "b1", "a3"),
    *("b2", "b1", "b4", "g-", "b2", "a4"),
    *("b3", "b2", "b5", "a4-", "b7", "b3"),
    *("b4", "b3", "b6", "b7", "b4", "a1"),
    *("b5", "b4", "b7-", "b7", "g", "b5"),
    *("b6", "a1", "b7", "g", "a4", "b5", "b6", "a4", "b6"),
)


def nt_dot(left, right):
    return lax.dot_general(left, right, (((1,), (1,)), ((), ())), preferred_element_type=F32)


def tn_dot(left, right):
    return lax.dot_general(left, right, (((0,), (0,)), ((), ())), preferred_element_type=F32)


def nn_dot(left, right):
    return jnp.dot(left, right, preferred_element_type=F32)


def xor_permute(value, axis, size, distance):
    return lax.ppermute(value, axis, [(d, d ^ distance) for d in range(size)])


def ordered_offsets(bits):
    offsets = [0]
    for bit in reversed(bits):
        offsets = [o | bit for o in offsets] + offsets
    return offsets


class Lane:
    def __init__(self, chain):
        self.chain = chain
        self.result = None
        self.request = next(chain)
        self.send(self.request[0])

    def send(self, value):
        self.value = xor_permute(value, *self.request[1:])
        self.request = None

    def advance(self, value, hold):
        if self.request is not None:
            self.send(value)
            return
        try:
            self.request = self.chain.send(value)
            self.value = self.request[0]
            if not hold:
                self.send(self.value)
        except StopIteration as end:
            self.result = end.value


class Cell:
    def __init__(self, value):
        self.value = value


class Timeline:
    def __init__(self):
        self.cells = []
        self.renewed = []

    def prepare(self, value):
        cell = Cell(value)
        self.cells.append(cell)
        return cell

    def fence(self, *lanes, hold=False):
        cells, self.cells = self.cells + self.renewed, []
        leaves, tree = jax.tree.flatten(
            ([lane.value for lane in lanes], [cell.value for cell in cells])
        )
        values, prepared = jax.tree.unflatten(tree, lax.optimization_barrier(tuple(leaves)))
        for cell, value in zip(cells, prepared):
            cell.value = value
        for lane, value in zip(lanes, values):
            lane.advance(value, hold)


def single(value, size, distance):
    arrived = yield value, "wa", size, distance
    return arrived


def gather_dev(block, size, distances):
    held = block[None]
    for distance in distances:
        arrived = yield held, "dev", size, distance
        held = jnp.concatenate([held, arrived], axis=0)
    return held


def sum_dev(value, size, distances):
    for distance in distances:
        arrived = yield value, "dev", size, distance
        value = value + arrived
    return value


def scatter_sum(away, kept, size, bits):
    for index, bit in enumerate(bits):
        arrived = yield away, "wa", size, bit
        total = kept.value.astype(F32) + arrived.astype(F32)
        if index + 1 < len(bits):
            half = total.shape[0] // 2
            total = total.astype(BF16)
            away, kept = total[:half], Cell(total[half:])
    return total


def packing(me, token_rows, tile_owner_adapter, tile_live_count):
    all_tiles = jnp.arange(tile_live_count.shape[0], dtype=jnp.int32)[:, None]
    row = jnp.arange(token_rows, dtype=jnp.int32)
    first_tile = me * (token_rows // TILE)
    tile_of_row = first_tile + row // TILE
    here = all_tiles == tile_of_row[None, :]
    before = (all_tiles >= first_tile) & (all_tiles < tile_of_row[None, :])
    live = jnp.sum(jnp.where(here, tile_live_count[:, None], 0), axis=0)
    begin = jnp.sum(jnp.where(before, tile_live_count[:, None], 0), axis=0)
    row_adapter = jnp.sum(jnp.where(here, tile_owner_adapter, 0), axis=0)
    position = row % TILE
    return jnp.where(position < live, begin + position, -1), row_adapter


def run(
    rows,
    wa_size,
    dev_size,
    output_gradient,
    down_weight,
    gate_preactivation,
    up_preactivation,
    adapter_down_factor,
    adapter_up_factor,
    tile_owner_adapter,
    tile_live_count,
):
    me = lax.axis_index("wa")
    dev = lax.axis_index("dev")
    token_rows = output_gradient.shape[0]
    hidden_local, group_width = down_weight.shape
    shard_columns = adapter_up_factor.shape[2]
    adapters, rank = adapter_down_factor.shape[:2]
    owned = adapters // wa_size
    sub_width = group_width // dev_size
    wa_bits = [1 << b for b in range(wa_size.bit_length() - 1)]
    dev_steps = [1 << b for b in reversed(range(dev_size.bit_length() - 1))]
    offsets = ordered_offsets(wa_bits)
    half = len(offsets) // 2
    time = Timeline()

    target, row_adapter = packing(me, token_rows, tile_owner_adapter, tile_live_count)
    pick = (jnp.arange(rows, dtype=jnp.int32)[:, None] == target[None, :]).astype(BF16)

    def compact(values):
        return nn_dot(pick, values).astype(BF16)

    flat_up = adapter_up_factor.reshape(adapters * rank, shard_columns)
    flat_down = adapter_down_factor.reshape(adapters * rank, hidden_local)

    def selector_for(order):
        return nn_dot(pick, (row_adapter[:, None] == order[None, :]).astype(BF16)).astype(BF16)

    selector = selector_for(jnp.arange(adapters, dtype=jnp.int32))

    def choose(values):
        wide = values.reshape(rows, adapters, rank) * selector.astype(F32)[:, :, None]
        return jnp.sum(wide, axis=1)

    def spread(values, which):
        wide = values[:, None, :] * which[:, :, None]
        return wide.reshape(rows, adapters * rank)

    def owner_spread(values, bits):
        place = jnp.arange(adapters, dtype=jnp.int32) // owned
        offset = sum(
            jnp.where((place >> (len(bits) - 1 - k)) & 1 == 0, bit, 0)
            for k, bit in enumerate(bits)
        )
        order = jnp.bitwise_xor(me, offset) * owned + jnp.arange(adapters, dtype=jnp.int32) % owned
        return spread(values, selector_for(order))

    masked = time.prepare(
        jnp.where(target[:, None] >= 0, output_gradient, jnp.zeros((), output_gradient.dtype))
    )
    time.fence()
    begins = [jnp.bitwise_xor(me, o) * group_width + dev * sub_width for o in offsets]
    pieces = [
        time.prepare(compact(lax.dynamic_slice_in_dim(masked.value, begin, sub_width, 1)))
        for begin in begins
    ]
    steps = len(dev_steps)
    grad_slice = compact(
        lax.dynamic_slice_in_dim(masked.value, dev * shard_columns, shard_columns, 1)
    )
    out_partial = time.prepare(choose(nt_dot(grad_slice, flat_up)))
    gate_all, up_all = time.prepare(gate_preactivation), time.prepare(up_preactivation)
    time.fence()
    out_lane = Lane(sum_dev(out_partial.value, dev_size, dev_steps))
    first_lanes = [Lane(single(pieces[k].value, wa_size, offsets[k])) for k in range(half)]
    gate = time.prepare(compact(gate_all.value))
    up = time.prepare(compact(up_all.value))
    hidden = time.prepare(
        (jax.nn.silu(gate.value.astype(F32)) * up.value.astype(F32)).astype(BF16)
    )
    time.fence(out_lane, *first_lanes)
    first = jnp.concatenate([lane.result for lane in first_lanes], axis=0)
    first_lane = Lane(gather_dev(first, dev_size, dev_steps))
    second_lanes = [
        Lane(single(pieces[k].value, wa_size, offsets[k])) for k in range(half, len(offsets) - 1)
    ]
    in_partial = time.prepare(choose(nt_dot(hidden.value, flat_down)))
    for _ in range(steps - 2):
        time.fence(out_lane)
    time.fence(out_lane, *second_lanes)
    lora_out = out_lane.result.astype(BF16)
    spread_out = time.prepare(spread(lora_out, selector))

    orders = {
        "y": wa_bits,
        "z": wa_bits[1:] + wa_bits[:1],
    }
    unit = hidden_local // 14
    kinds, spans, at = {}, {}, {"a": 0, "b": 0}
    for name, kind, width in PLAN:
        kinds[name] = orders[kind]
        begin = at.get(name[0], 0)
        spans[name] = slice(begin * unit, (begin + width) * unit)
        at[name[0]] = begin + width
    ready, lanes = {}, {}

    def ready_adapter(name, values, others):
        partial = tn_dot(owner_spread(values, kinds[name]), others).astype(BF16)
        middle = partial.shape[0] // 2
        ready[name] = time.prepare(partial[:middle]), time.prepare(partial[middle:])

    def launch(name):
        away, own = ready[name]
        lanes[name] = Lane(scatter_sum(away.value, own, wa_size, kinds[name]))

    second = jnp.concatenate([lane.result for lane in second_lanes] + [pieces[-1].value], axis=0)
    second_lane = Lane(gather_dev(second, dev_size, dev_steps))
    ready_adapter("a0", lora_out, hidden.value[:, spans["a0"]])
    ready_adapter("a1", lora_out, hidden.value[:, spans["a1"]])
    launch("a0")
    launch("a1")
    time.renewed = [hidden, spread_out]
    time.fence(first_lane)
    ready_adapter("a2", lora_out, hidden.value[:, spans["a2"]])
    time.fence(second_lane, lanes["a0"], lanes["a1"])
    launch("a2")
    for _ in range(steps - 2):
        time.fence(first_lane, second_lane)
    time.fence(first_lane, second_lane, lanes["a2"])
    in_lane = Lane(sum_dev(in_partial.value, dev_size, dev_steps))

    def place_of(offset):
        bits = [
            ((offset >> (step.bit_length() - 1)) & 1) * (dev_size // (2 * step))
            for step in dev_steps
        ]
        return sum(bits)

    def assemble(lane):
        held = lane.result
        parts = [
            lax.dynamic_index_in_dim(held, place_of(jnp.bitwise_xor(dev, j)), 0, keepdims=False)
            for j in range(dev_size)
        ]
        return jnp.concatenate(parts, axis=1)

    columns_away, columns_own = Cell(assemble(first_lane)), Cell(assemble(second_lane))
    time.renewed += [columns_away, columns_own]

    def columns_for(bits):
        if bits == wa_bits:
            return columns_away.value, columns_own.value
        blocks = {}
        for k, offset in enumerate(offsets):
            part = columns_away.value if k < half else columns_own.value
            blocks[offset] = part[(k % half) * rows : (k % half + 1) * rows]
        order = [blocks[offset] for offset in ordered_offsets(bits)]
        return jnp.concatenate(order[:half], axis=0), jnp.concatenate(order[half:], axis=0)

    def make_ready(name):
        if name in ready:
            return
        if name == "g":
            ready_adapter(name, in_lane.result.astype(BF16), grad_slice)
            return
        if name[0] == "a":
            ready_adapter(name, lora_out, hidden.value[:, spans[name]])
            return
        weights = down_weight[spans[name]]
        ready[name] = tuple(
            time.prepare(nt_dot(part, weights).astype(BF16)) for part in columns_for(kinds[name])
        )

    def finish(name):
        span = spans[name]
        hidden_grad = lanes[name].result + 2.0 * nn_dot(spread_out.value, flat_down[:, span])
        gate_here, up_here = gate.value[:, span].astype(F32), up.value[:, span].astype(F32)
        sigmoid = jax.nn.sigmoid(gate_here)
        grad_up = (hidden_grad * gate_here * sigmoid).astype(BF16)
        grad_gate = (
            hidden_grad * up_here * sigmoid * (1.0 + gate_here * (1.0 - sigmoid))
        ).astype(BF16)
        return time.prepare(
            (tn_dot(pick, grad_gate).astype(BF16), tn_dot(pick, grad_up).astype(BF16))
        )

    done = {}
    names = [event[:2].rstrip("-") for event in EVENTS]
    for index, name in enumerate(names):
        for soon in names[index : index + 3]:
            make_ready(soon)
        if name not in lanes:
            time.fence()
            launch(name)
            while index == 0 and in_lane.result is None:
                time.fence(in_lane)
            continue
        lane = lanes[name]
        time.fence(lane, hold=EVENTS[index].endswith("-"))
        while lane.result is None and name not in names[index + 1 :]:
            time.fence(lane)
        if lane.result is not None:
            done[name] = finish(name) if name[0] == "b" else Cell(2.0 * lane.result)

    def joined(letter, index=None):
        names = sorted(name for name in done if name[0] == letter)
        values = [done[name].value for name in names]
        return jnp.concatenate(values if index is None else [v[index] for v in values], axis=1)

    return (
        joined("b", 0),
        joined("b", 1),
        joined("a").reshape(owned, rank, hidden_local),
        joined("g").reshape(owned, rank, shard_columns),
    )


def add_rest(
    rows,
    outputs,
    output_gradient,
    down_weight,
    gate_preactivation,
    up_preactivation,
    adapter_down_factor,
    adapter_up_factor,
    tile_owner_adapter,
    tile_live_count,
):
    grad_gate, grad_up, grad_a, grad_b = outputs
    me = lax.axis_index("wa")
    dev = lax.axis_index("dev")
    token_rows = output_gradient.shape[0]
    rest = token_rows - rows
    shard_columns = adapter_up_factor.shape[2]
    adapters, rank = adapter_down_factor.shape[:2]
    target, row_adapter = packing(me, token_rows, tile_owner_adapter, tile_live_count)
    numbers = rows + jnp.arange(rest, dtype=jnp.int32)
    pick = (numbers[:, None] == target[None, :]).astype(BF16)
    owner = row_adapter[:, None] == jnp.arange(adapters, dtype=jnp.int32)[None, :]
    selector = nn_dot(pick, owner.astype(BF16))
    flat_down = adapter_down_factor.reshape(adapters * rank, -1)
    flat_up = adapter_up_factor.reshape(adapters * rank, -1)

    def choose(values):
        return jnp.sum(values.reshape(rest, adapters, rank) * selector[:, :, None], axis=1)

    def spread(values):
        wide = values[:, None, :] * selector.astype(BF16)[:, :, None]
        return wide.reshape(rest, adapters * rank)

    masked = nn_dot(pick, output_gradient).astype(BF16)
    gate = nn_dot(pick, gate_preactivation)
    up = nn_dot(pick, up_preactivation)
    hidden = (jax.nn.silu(gate) * up).astype(BF16)
    exchanged = lax.all_to_all(masked, "wa", split_axis=1, concat_axis=0, tiled=True)
    partial = nt_dot(exchanged, down_weight).astype(BF16)
    base = lax.psum_scatter(partial, "wa", scatter_dimension=0, tiled=True).astype(F32)
    columns = lax.dynamic_slice_in_dim(masked, dev * shard_columns, shard_columns, 1)
    lora_in, lora_out = lax.psum(
        (choose(nt_dot(hidden, flat_down)), choose(nt_dot(columns, flat_up))), "dev"
    )
    spread_in, spread_out = spread(lora_in.astype(BF16)), spread(lora_out.astype(BF16))
    hidden_grad = base + 2.0 * nn_dot(spread_out, flat_down)
    sigmoid = jax.nn.sigmoid(gate)
    more_up = (hidden_grad * gate * sigmoid).astype(BF16)
    more_gate = (hidden_grad * up * sigmoid * (1.0 + gate * (1.0 - sigmoid))).astype(BF16)

    def owner_sum(wide, values):
        partial = (2.0 * tn_dot(wide, values)).reshape(adapters, rank, -1)
        return lax.psum_scatter(partial, "wa", scatter_dimension=0, tiled=True)

    return (
        grad_gate + tn_dot(pick, more_gate).astype(BF16),
        grad_up + tn_dot(pick, more_up).astype(BF16),
        grad_a + owner_sum(spread_out, hidden),
        grad_b + owner_sum(spread_in, columns),
    )


def solution(mesh):
    wa_size, dev_size = mesh.shape["wa"], mesh.shape["dev"]

    def on_device(*inputs):
        token_rows = inputs[0].shape[0]
        live = inputs[-1]
        rows = token_rows * ROWS // 16
        tile = jnp.arange(live.shape[0], dtype=jnp.int32)[:, None]
        shard = jnp.arange(wa_size, dtype=jnp.int32)[None, :]
        here = tile // (live.shape[0] // wa_size) == shard
        totals = jnp.sum(jnp.where(here, live[:, None], 0), axis=0)
        left = jnp.max(totals) - rows
        outputs = run(rows, wa_size, dev_size, *inputs)

        return lax.cond(
            left > 0,
            lambda *state: add_rest(rows, state[:4], *state[4:]),
            lambda *state: state[:4],
            *outputs,
            *inputs,
        )

    placed = (
        P("wa", None),
        P("dev", "wa"),
        P("wa", "dev"),
        P("wa", "dev"),
        P(None, None, "dev"),
        P(None, None, "dev"),
        P(),
        P(),
    )
    return jax.shard_map(
        on_device,
        mesh=mesh,
        in_specs=placed,
        out_specs=(P("wa", "dev"), P("wa", "dev"), P("wa", None, "dev"), P("wa", None, "dev")),
        check_vma=False,
    )
```

```python
import functools

import jax
import jax.numpy as jnp
from jax import lax
from jax.sharding import PartitionSpec as P

TILE = 16
BF16 = jnp.bfloat16
F32 = jnp.float32

ROWS = (12, 13, 16)

PLAN = (
    ("a0", "y", 4),
    ("a1", "z", 5),
    ("a2", "y", 5),
    ("b0", "y", 2),
    ("b1", "y", 4),
    ("b2", "y", 4),
    ("b3", "y", 2),
    ("b4", "y", 1),
    ("b5", "z", 1),
    ("g", "z", 0),
)
EVENTS = (
    *("b0", "a0", "a1-", "g", "a2", "a0", "b1", "g-", "a2", "b5"),
    *("b0", "a2", "b2", "g", "b5", "b0", "g-", "b5-", "b0"),
    *("b1", "a1", "b3", "b1", "b1"),
    *("b2", "b4", "a1", "g", "b2", "b3", "b5", "b3", "b2"),
    *("b4", "g", "b5", "b3", "b4", "b4"),
)


def nt_dot(left, right):
    return lax.dot_general(left, right, (((1,), (1,)), ((), ())), preferred_element_type=F32)


def tn_dot(left, right):
    return lax.dot_general(left, right, (((0,), (0,)), ((), ())), preferred_element_type=F32)


def nn_dot(left, right):
    return jnp.dot(left, right, preferred_element_type=F32)


def xor_permute(value, axis, size, distance):
    return lax.ppermute(value, axis, [(d, d ^ distance) for d in range(size)])


def ordered_offsets(bits):
    offsets = [0]
    for bit in reversed(bits):
        offsets = [o | bit for o in offsets] + offsets
    return offsets


class Lane:
    def __init__(self, chain):
        self.chain = chain
        self.result = None
        self.request = next(chain)
        self.send(self.request[0])

    def send(self, value):
        self.value = xor_permute(value, *self.request[1:])
        self.request = None

    def advance(self, value, hold):
        if self.request is not None:
            self.send(value)
            return
        try:
            self.request = self.chain.send(value)
            self.value = self.request[0]
            if not hold:
                self.send(self.value)
        except StopIteration as end:
            self.result = end.value


class Cell:
    def __init__(self, value):
        self.value = value


class Timeline:
    def __init__(self):
        self.cells = []
        self.renewed = []

    def prepare(self, value):
        cell = Cell(value)
        self.cells.append(cell)
        return cell

    def fence(self, *lanes, hold=False):
        cells, self.cells = self.cells + self.renewed, []
        leaves, tree = jax.tree.flatten(
            ([lane.value for lane in lanes], [cell.value for cell in cells])
        )
        values, prepared = jax.tree.unflatten(tree, lax.optimization_barrier(tuple(leaves)))
        for cell, value in zip(cells, prepared):
            cell.value = value
        for lane, value in zip(lanes, values):
            lane.advance(value, hold)


def single(value, size, distance):
    arrived = yield value, "wa", size, distance
    return arrived


def gather_dev(block, size, distances):
    held = block[None]
    for distance in distances:
        arrived = yield held, "dev", size, distance
        held = jnp.concatenate([held, arrived], axis=0)
    return held


def sum_dev(value, size, distances):
    for distance in distances:
        arrived = yield value, "dev", size, distance
        value = value + arrived
    return value


def scatter_sum(away, kept, size, bits):
    for index, bit in enumerate(bits):
        arrived = yield away, "wa", size, bit
        total = kept.value.astype(F32) + arrived.astype(F32)
        if index + 1 < len(bits):
            half = total.shape[0] // 2
            total = total.astype(BF16)
            away, kept = total[:half], Cell(total[half:])
    return total


def packing(me, token_rows, tile_owner_adapter, tile_live_count):
    all_tiles = jnp.arange(tile_live_count.shape[0], dtype=jnp.int32)[:, None]
    row = jnp.arange(token_rows, dtype=jnp.int32)
    first_tile = me * (token_rows // TILE)
    tile_of_row = first_tile + row // TILE
    here = all_tiles == tile_of_row[None, :]
    before = (all_tiles >= first_tile) & (all_tiles < tile_of_row[None, :])
    live = jnp.sum(jnp.where(here, tile_live_count[:, None], 0), axis=0)
    begin = jnp.sum(jnp.where(before, tile_live_count[:, None], 0), axis=0)
    row_adapter = jnp.sum(jnp.where(here, tile_owner_adapter, 0), axis=0)
    position = row % TILE
    return jnp.where(position < live, begin + position, -1), row_adapter


def run(
    rows,
    wa_size,
    dev_size,
    output_gradient,
    down_weight,
    gate_preactivation,
    up_preactivation,
    adapter_down_factor,
    adapter_up_factor,
    tile_owner_adapter,
    tile_live_count,
):
    me = lax.axis_index("wa")
    dev = lax.axis_index("dev")
    token_rows = output_gradient.shape[0]
    hidden_local, group_width = down_weight.shape
    shard_columns = adapter_up_factor.shape[2]
    adapters, rank = adapter_down_factor.shape[:2]
    owned = adapters // wa_size
    sub_width = group_width // dev_size
    wa_bits = [1 << b for b in range(wa_size.bit_length() - 1)]
    dev_steps = [1 << b for b in reversed(range(dev_size.bit_length() - 1))]
    offsets = ordered_offsets(wa_bits)
    half = len(offsets) // 2
    time = Timeline()

    target, row_adapter = packing(me, token_rows, tile_owner_adapter, tile_live_count)
    pick = (jnp.arange(rows, dtype=jnp.int32)[:, None] == target[None, :]).astype(BF16)

    def compact(values):
        return nn_dot(pick, values).astype(BF16)

    flat_up = adapter_up_factor.reshape(adapters * rank, shard_columns)
    flat_down = adapter_down_factor.reshape(adapters * rank, hidden_local)

    def selector_for(order):
        return nn_dot(pick, (row_adapter[:, None] == order[None, :]).astype(BF16)).astype(BF16)

    selector = selector_for(jnp.arange(adapters, dtype=jnp.int32))

    def choose(values):
        wide = values.reshape(rows, adapters, rank) * selector.astype(F32)[:, :, None]
        return jnp.sum(wide, axis=1)

    def spread(values, which):
        wide = values[:, None, :] * which[:, :, None]
        return wide.reshape(rows, adapters * rank)

    def owner_spread(values, bits):
        place = jnp.arange(adapters, dtype=jnp.int32) // owned
        offset = sum(
            jnp.where((place >> (len(bits) - 1 - k)) & 1 == 0, bit, 0)
            for k, bit in enumerate(bits)
        )
        order = jnp.bitwise_xor(me, offset) * owned + jnp.arange(adapters, dtype=jnp.int32) % owned
        return spread(values, selector_for(order))

    masked = time.prepare(
        jnp.where(target[:, None] >= 0, output_gradient, jnp.zeros((), output_gradient.dtype))
    )
    time.fence()
    begins = [jnp.bitwise_xor(me, o) * group_width + dev * sub_width for o in offsets]
    pieces = [
        time.prepare(compact(lax.dynamic_slice_in_dim(masked.value, begin, sub_width, 1)))
        for begin in begins
    ]
    steps = len(dev_steps)
    grad_slice = compact(
        lax.dynamic_slice_in_dim(masked.value, dev * shard_columns, shard_columns, 1)
    )
    out_partial = time.prepare(choose(nt_dot(grad_slice, flat_up)))
    gate_all, up_all = time.prepare(gate_preactivation), time.prepare(up_preactivation)
    time.fence()
    out_lane = Lane(sum_dev(out_partial.value, dev_size, dev_steps))
    first_lanes = [Lane(single(pieces[k].value, wa_size, offsets[k])) for k in range(half)]
    gate = time.prepare(compact(gate_all.value))
    up = time.prepare(compact(up_all.value))
    hidden = time.prepare(
        (jax.nn.silu(gate.value.astype(F32)) * up.value.astype(F32)).astype(BF16)
    )
    time.fence(out_lane, *first_lanes)
    first = jnp.concatenate([lane.result for lane in first_lanes], axis=0)
    first_lane = Lane(gather_dev(first, dev_size, dev_steps))
    second_lanes = [
        Lane(single(pieces[k].value, wa_size, offsets[k])) for k in range(half, len(offsets) - 1)
    ]
    in_partial = time.prepare(choose(nt_dot(hidden.value, flat_down)))
    for _ in range(steps - 2):
        time.fence(out_lane)
    time.fence(out_lane, *second_lanes)
    lora_out = out_lane.result.astype(BF16)
    spread_out = time.prepare(spread(lora_out, selector))

    orders = {
        "y": wa_bits,
        "z": wa_bits[1:] + wa_bits[:1],
    }
    unit = hidden_local // 14
    kinds, spans, at = {}, {}, {"a": 0, "b": 0}
    for name, kind, width in PLAN:
        kinds[name] = orders[kind]
        begin = at.get(name[0], 0)
        spans[name] = slice(begin * unit, (begin + width) * unit)
        at[name[0]] = begin + width
    ready, lanes = {}, {}

    def ready_adapter(name, values, others):
        partial = tn_dot(owner_spread(values, kinds[name]), others).astype(BF16)
        middle = partial.shape[0] // 2
        ready[name] = time.prepare(partial[:middle]), time.prepare(partial[middle:])

    def launch(name):
        away, own = ready[name]
        lanes[name] = Lane(scatter_sum(away.value, own, wa_size, kinds[name]))

    second = jnp.concatenate([lane.result for lane in second_lanes] + [pieces[-1].value], axis=0)
    second_lane = Lane(gather_dev(second, dev_size, dev_steps))
    ready_adapter("a0", lora_out, hidden.value[:, spans["a0"]])
    ready_adapter("a1", lora_out, hidden.value[:, spans["a1"]])
    launch("a0")
    launch("a1")
    time.renewed = [hidden, spread_out]
    for _ in range(steps - 1):
        time.fence(first_lane)
    ready_adapter("a2", lora_out, hidden.value[:, spans["a2"]])
    time.fence(first_lane, second_lane, lanes["a0"])
    launch("a2")
    for _ in range(steps - 2):
        time.fence(second_lane)
    time.fence(second_lane, lanes["a1"])
    in_lane = Lane(sum_dev(in_partial.value, dev_size, dev_steps))

    def place_of(offset):
        bits = [
            ((offset >> (step.bit_length() - 1)) & 1) * (dev_size // (2 * step))
            for step in dev_steps
        ]
        return sum(bits)

    def assemble(lane):
        held = lane.result
        parts = [
            lax.dynamic_index_in_dim(held, place_of(jnp.bitwise_xor(dev, j)), 0, keepdims=False)
            for j in range(dev_size)
        ]
        return jnp.concatenate(parts, axis=1)

    columns_away, columns_own = Cell(assemble(first_lane)), Cell(assemble(second_lane))
    time.renewed += [columns_away, columns_own]

    def columns_for(bits):
        if bits == wa_bits:
            return columns_away.value, columns_own.value
        blocks = {}
        for k, offset in enumerate(offsets):
            part = columns_away.value if k < half else columns_own.value
            blocks[offset] = part[(k % half) * rows : (k % half + 1) * rows]
        order = [blocks[offset] for offset in ordered_offsets(bits)]
        return jnp.concatenate(order[:half], axis=0), jnp.concatenate(order[half:], axis=0)

    def make_ready(name):
        if name in ready:
            return
        if name == "g":
            ready_adapter(name, in_lane.result.astype(BF16), grad_slice)
            return
        if name[0] == "a":
            ready_adapter(name, lora_out, hidden.value[:, spans[name]])
            return
        weights = down_weight[spans[name]]
        ready[name] = tuple(
            time.prepare(nt_dot(part, weights).astype(BF16)) for part in columns_for(kinds[name])
        )

    def finish(name):
        span = spans[name]
        hidden_grad = lanes[name].result + 2.0 * nn_dot(spread_out.value, flat_down[:, span])
        gate_here, up_here = gate.value[:, span].astype(F32), up.value[:, span].astype(F32)
        sigmoid = jax.nn.sigmoid(gate_here)
        grad_up = (hidden_grad * gate_here * sigmoid).astype(BF16)
        grad_gate = (
            hidden_grad * up_here * sigmoid * (1.0 + gate_here * (1.0 - sigmoid))
        ).astype(BF16)
        return time.prepare(
            (tn_dot(pick, grad_gate).astype(BF16), tn_dot(pick, grad_up).astype(BF16))
        )

    done = {}
    names = [event[:2].rstrip("-") for event in EVENTS]
    for index, name in enumerate(names):
        for soon in names[index : index + 3]:
            make_ready(soon)
        if name not in lanes:
            time.fence()
            launch(name)
            while index == 0 and in_lane.result is None:
                time.fence(in_lane)
            continue
        lane = lanes[name]
        time.fence(lane, hold=EVENTS[index].endswith("-"))
        while lane.result is None and name not in names[index + 1 :]:
            time.fence(lane)
        if lane.result is not None:
            done[name] = finish(name) if name[0] == "b" else Cell(2.0 * lane.result)

    def joined(letter, index=None):
        names = sorted(name for name in done if name[0] == letter)
        values = [done[name].value for name in names]
        return jnp.concatenate(values if index is None else [v[index] for v in values], axis=1)

    return (
        joined("b", 0),
        joined("b", 1),
        joined("a").reshape(owned, rank, hidden_local),
        joined("g").reshape(owned, rank, shard_columns),
    )


def solution(mesh):
    wa_size, dev_size = mesh.shape["wa"], mesh.shape["dev"]

    def on_device(*inputs):
        live = inputs[-1]
        sizes = [inputs[0].shape[0] * part // 16 for part in ROWS]
        tile = jnp.arange(live.shape[0], dtype=jnp.int32)[:, None]
        shard = jnp.arange(wa_size, dtype=jnp.int32)[None, :]
        here = tile // (live.shape[0] // wa_size) == shard
        totals = jnp.sum(jnp.where(here, live[:, None], 0), axis=0)
        above = sum((totals > size).astype(jnp.int32) for size in sizes[:-1])
        programs = [functools.partial(run, size, wa_size, dev_size) for size in sizes]
        return lax.switch(jnp.max(above), programs, *inputs)

    placed = (
        P("wa", None),
        P("dev", "wa"),
        P("wa", "dev"),
        P("wa", "dev"),
        P(None, None, "dev"),
        P(None, None, "dev"),
        P(),
        P(),
    )
    return jax.shard_map(
        on_device,
        mesh=mesh,
        in_specs=placed,
        out_specs=(P("wa", "dev"), P("wa", "dev"), P("wa", None, "dev"), P("wa", None, "dev")),
        check_vma=False,
    )
```

```python
import functools

import jax
import jax.numpy as jnp
from jax import lax
from jax.sharding import PartitionSpec as P

TILE = 16
BF16 = jnp.bfloat16
F32 = jnp.float32

ROWS = (12, 13, 16)

PLAN = (
    ("a0", "y", 2),
    ("a1", "z", 2),
    ("a2", "y", 5),
    ("a3", "z", 5),
    ("b0", "y", 2),
    ("b1", "y", 3),
    ("b2", "y", 3),
    ("b3", "y", 2),
    ("b4", "y", 2),
    ("b5", "y", 1),
    ("b6", "z", 1),
    ("g", "y", 0),
)
EVENTS = (
    *("a1", "a3", "b0", "a0", "a1", "a0", "b1", "a2", "a3", "b0", "a1", "a2"),
    *("a3", "b0", "b2", "b1", "b0", "b6", "a2", "b3", "b1", "b2", "b6", "b1"),
    *("b4", "b3", "b2", "a3", "g", "b4", "b2", "b6", "b3", "b5", "g", "b4"),
    *("b5", "g", "b5", "b6", "b4", "b3", "g", "b5"),
)


def nt_dot(left, right):
    return lax.dot_general(left, right, (((1,), (1,)), ((), ())), preferred_element_type=F32)


def tn_dot(left, right):
    return lax.dot_general(left, right, (((0,), (0,)), ((), ())), preferred_element_type=F32)


def nn_dot(left, right):
    return jnp.dot(left, right, preferred_element_type=F32)


def xor_permute(value, axis, size, distance):
    return lax.ppermute(value, axis, [(d, d ^ distance) for d in range(size)])


def ordered_offsets(bits):
    offsets = [0]
    for bit in reversed(bits):
        offsets = [o | bit for o in offsets] + offsets
    return offsets


class Lane:
    def __init__(self, chain):
        self.chain = chain
        self.result = None
        self.request = next(chain)
        self.send(self.request[0])

    def send(self, value):
        self.value = xor_permute(value, *self.request[1:])
        self.request = None

    def advance(self, value, hold):
        if self.request is not None:
            self.send(value)
            return
        try:
            self.request = self.chain.send(value)
            self.value = self.request[0]
            if not hold:
                self.send(self.value)
        except StopIteration as end:
            self.result = end.value


class Cell:
    def __init__(self, value):
        self.value = value


class Timeline:
    def __init__(self):
        self.cells = []
        self.renewed = []

    def prepare(self, value):
        cell = Cell(value)
        self.cells.append(cell)
        return cell

    def fence(self, *lanes, hold=False):
        cells, self.cells = self.cells + self.renewed, []
        leaves, tree = jax.tree.flatten(
            ([lane.value for lane in lanes], [cell.value for cell in cells])
        )
        values, prepared = jax.tree.unflatten(tree, lax.optimization_barrier(tuple(leaves)))
        for cell, value in zip(cells, prepared):
            cell.value = value
        for lane, value in zip(lanes, values):
            lane.advance(value, hold)


def single(value, size, distance):
    arrived = yield value, "wa", size, distance
    return arrived


def gather_dev(block, size, distances):
    held = block[None]
    for distance in distances:
        arrived = yield held, "dev", size, distance
        held = jnp.concatenate([held, arrived], axis=0)
    return held


def sum_dev(value, size, distances):
    for distance in distances:
        arrived = yield value, "dev", size, distance
        value = value + arrived
    return value


def scatter_sum(away, kept, size, bits):
    for index, bit in enumerate(bits):
        arrived = yield away, "wa", size, bit
        total = kept.value.astype(F32) + arrived.astype(F32)
        if index + 1 < len(bits):
            half = total.shape[0] // 2
            total = total.astype(BF16)
            away, kept = total[:half], Cell(total[half:])
    return total


def packing(me, token_rows, tile_owner_adapter, tile_live_count):
    all_tiles = jnp.arange(tile_live_count.shape[0], dtype=jnp.int32)[:, None]
    row = jnp.arange(token_rows, dtype=jnp.int32)
    first_tile = me * (token_rows // TILE)
    tile_of_row = first_tile + row // TILE
    here = all_tiles == tile_of_row[None, :]
    before = (all_tiles >= first_tile) & (all_tiles < tile_of_row[None, :])
    live = jnp.sum(jnp.where(here, tile_live_count[:, None], 0), axis=0)
    begin = jnp.sum(jnp.where(before, tile_live_count[:, None], 0), axis=0)
    row_adapter = jnp.sum(jnp.where(here, tile_owner_adapter, 0), axis=0)
    position = row % TILE
    return jnp.where(position < live, begin + position, -1), row_adapter


def run(
    rows,
    wa_size,
    dev_size,
    output_gradient,
    down_weight,
    gate_preactivation,
    up_preactivation,
    adapter_down_factor,
    adapter_up_factor,
    tile_owner_adapter,
    tile_live_count,
):
    me = lax.axis_index("wa")
    dev = lax.axis_index("dev")
    token_rows = output_gradient.shape[0]
    hidden_local, group_width = down_weight.shape
    shard_columns = adapter_up_factor.shape[2]
    adapters, rank = adapter_down_factor.shape[:2]
    owned = adapters // wa_size
    sub_width = group_width // dev_size
    wa_bits = [1 << b for b in range(wa_size.bit_length() - 1)]
    dev_steps = [1 << b for b in reversed(range(dev_size.bit_length() - 1))]
    offsets = ordered_offsets(wa_bits)
    half = len(offsets) // 2
    time = Timeline()

    target, row_adapter = packing(me, token_rows, tile_owner_adapter, tile_live_count)
    pick = (jnp.arange(rows, dtype=jnp.int32)[:, None] == target[None, :]).astype(BF16)

    def compact(values):
        return nn_dot(pick, values).astype(BF16)

    flat_up = adapter_up_factor.reshape(adapters * rank, shard_columns)
    flat_down = adapter_down_factor.reshape(adapters * rank, hidden_local)

    def selector_for(order):
        return nn_dot(pick, (row_adapter[:, None] == order[None, :]).astype(BF16)).astype(BF16)

    selector = selector_for(jnp.arange(adapters, dtype=jnp.int32))

    def choose(values):
        wide = values.reshape(rows, adapters, rank) * selector.astype(F32)[:, :, None]
        return jnp.sum(wide, axis=1)

    def spread(values, which):
        wide = values[:, None, :] * which[:, :, None]
        return wide.reshape(rows, adapters * rank)

    def owner_spread(values, bits):
        place = jnp.arange(adapters, dtype=jnp.int32) // owned
        offset = sum(
            jnp.where((place >> (len(bits) - 1 - k)) & 1 == 0, bit, 0)
            for k, bit in enumerate(bits)
        )
        order = jnp.bitwise_xor(me, offset) * owned + jnp.arange(adapters, dtype=jnp.int32) % owned
        return spread(values, selector_for(order))

    gradient = time.prepare(compact(output_gradient))
    time.fence()
    begins = [jnp.bitwise_xor(me, o) * group_width + dev * sub_width for o in offsets]
    pieces = [
        time.prepare(lax.dynamic_slice_in_dim(gradient.value, begin, sub_width, 1))
        for begin in begins
    ]
    steps = len(dev_steps)
    grad_slice = lax.dynamic_slice_in_dim(gradient.value, dev * shard_columns, shard_columns, 1)
    out_partial = time.prepare(choose(nt_dot(grad_slice, flat_up)))
    gate_all, up_all = time.prepare(gate_preactivation), time.prepare(up_preactivation)
    time.fence()
    out_lane = Lane(sum_dev(out_partial.value, dev_size, dev_steps))
    first_lanes = [Lane(single(pieces[k].value, wa_size, offsets[k])) for k in range(half)]
    gate = time.prepare(compact(gate_all.value))
    up = time.prepare(compact(up_all.value))
    hidden = time.prepare(
        (jax.nn.silu(gate.value.astype(F32)) * up.value.astype(F32)).astype(BF16)
    )
    time.fence(out_lane, *first_lanes)
    first = jnp.concatenate([lane.result for lane in first_lanes], axis=0)
    first_lane = Lane(gather_dev(first, dev_size, dev_steps))
    second_lanes = [
        Lane(single(pieces[k].value, wa_size, offsets[k])) for k in range(half, len(offsets) - 1)
    ]
    in_partial = time.prepare(choose(nt_dot(hidden.value, flat_down)))
    for _ in range(steps - 2):
        time.fence(out_lane)
    time.fence(out_lane, *second_lanes)
    lora_out = out_lane.result.astype(BF16)
    spread_out = time.prepare(spread(lora_out, selector))

    orders = {
        "y": wa_bits,
        "z": wa_bits[1:] + wa_bits[:1],
    }
    unit = hidden_local // 14
    kinds, spans, at = {}, {}, {"a": 0, "b": 0}
    for name, kind, width in PLAN:
        kinds[name] = orders[kind]
        begin = at.get(name[0], 0)
        spans[name] = slice(begin * unit, (begin + width) * unit)
        at[name[0]] = begin + width
    ready, lanes = {}, {}

    def ready_adapter(name, values, others):
        partial = tn_dot(owner_spread(values, kinds[name]), others).astype(BF16)
        middle = partial.shape[0] // 2
        ready[name] = time.prepare(partial[:middle]), time.prepare(partial[middle:])

    def launch(name):
        away, own = ready[name]
        lanes[name] = Lane(scatter_sum(away.value, own, wa_size, kinds[name]))

    second = jnp.concatenate([lane.result for lane in second_lanes] + [pieces[-1].value], axis=0)
    second_lane = Lane(gather_dev(second, dev_size, dev_steps))
    for name in ("a0", "a1", "a2"):
        ready_adapter(name, lora_out, hidden.value[:, spans[name]])
        launch(name)
    time.renewed = [hidden, spread_out]
    for _ in range(steps - 1):
        time.fence(first_lane)
        time.fence(second_lane)
    time.fence(lanes["a0"])
    time.fence(first_lane, second_lane)
    in_lane = Lane(sum_dev(in_partial.value, dev_size, dev_steps))

    def place_of(offset):
        bits = [
            ((offset >> (step.bit_length() - 1)) & 1) * (dev_size // (2 * step))
            for step in dev_steps
        ]
        return sum(bits)

    def assemble(lane):
        held = lane.result
        parts = [
            lax.dynamic_index_in_dim(held, place_of(jnp.bitwise_xor(dev, j)), 0, keepdims=False)
            for j in range(dev_size)
        ]
        return jnp.concatenate(parts, axis=1)

    columns_away, columns_own = Cell(assemble(first_lane)), Cell(assemble(second_lane))
    time.renewed += [columns_away, columns_own]

    def columns_for(bits):
        if bits == wa_bits:
            return columns_away.value, columns_own.value
        blocks = {}
        for k, offset in enumerate(offsets):
            part = columns_away.value if k < half else columns_own.value
            blocks[offset] = part[(k % half) * rows : (k % half + 1) * rows]
        order = [blocks[offset] for offset in ordered_offsets(bits)]
        return jnp.concatenate(order[:half], axis=0), jnp.concatenate(order[half:], axis=0)

    def make_ready(name):
        if name in ready:
            return
        if name == "g":
            ready_adapter(name, in_lane.result.astype(BF16), grad_slice)
            return
        if name[0] == "a":
            ready_adapter(name, lora_out, hidden.value[:, spans[name]])
            return
        weights = down_weight[spans[name]]
        ready[name] = tuple(
            time.prepare(nt_dot(part, weights).astype(BF16)) for part in columns_for(kinds[name])
        )

    def finish(name):
        span = spans[name]
        hidden_grad = lanes[name].result + 2.0 * nn_dot(spread_out.value, flat_down[:, span])
        gate_here, up_here = gate.value[:, span].astype(F32), up.value[:, span].astype(F32)
        sigmoid = jax.nn.sigmoid(gate_here)
        grad_up = (hidden_grad * gate_here * sigmoid).astype(BF16)
        grad_gate = (
            hidden_grad * up_here * sigmoid * (1.0 + gate_here * (1.0 - sigmoid))
        ).astype(BF16)
        return time.prepare(
            (tn_dot(pick, grad_gate).astype(BF16), tn_dot(pick, grad_up).astype(BF16))
        )

    done = {}
    names = [event[:2].rstrip("-") for event in EVENTS]
    for index, name in enumerate(names):
        for soon in names[index : index + 3]:
            make_ready(soon)
        if name not in lanes:
            time.fence()
            launch(name)
            while name == "b1" and in_lane.result is None:
                time.fence(in_lane)
            continue
        lane = lanes[name]
        time.fence(lane, hold=EVENTS[index].endswith("-"))
        while lane.result is None and name not in names[index + 1 :]:
            time.fence(lane)
        if lane.result is not None:
            done[name] = finish(name) if name[0] == "b" else Cell(2.0 * lane.result)

    def joined(letter, index=None):
        names = sorted(name for name in done if name[0] == letter)
        values = [done[name].value for name in names]
        return jnp.concatenate(values if index is None else [v[index] for v in values], axis=1)

    return (
        joined("b", 0),
        joined("b", 1),
        joined("a").reshape(owned, rank, hidden_local),
        joined("g").reshape(owned, rank, shard_columns),
    )


def solution(mesh):
    wa_size, dev_size = mesh.shape["wa"], mesh.shape["dev"]

    def on_device(*inputs):
        live = inputs[-1]
        sizes = [inputs[0].shape[0] * part // 16 for part in ROWS]
        tile = jnp.arange(live.shape[0], dtype=jnp.int32)[:, None]
        shard = jnp.arange(wa_size, dtype=jnp.int32)[None, :]
        here = tile // (live.shape[0] // wa_size) == shard
        totals = jnp.sum(jnp.where(here, live[:, None], 0), axis=0)
        above = sum((totals > size).astype(jnp.int32) for size in sizes[:-1])
        programs = [functools.partial(run, size, wa_size, dev_size) for size in sizes]
        return lax.switch(jnp.max(above), programs, *inputs)

    placed = (
        P("wa", None),
        P("dev", "wa"),
        P("wa", "dev"),
        P("wa", "dev"),
        P(None, None, "dev"),
        P(None, None, "dev"),
        P(),
        P(),
    )
    return jax.shard_map(
        on_device,
        mesh=mesh,
        in_specs=placed,
        out_specs=(P("wa", "dev"), P("wa", "dev"), P("wa", None, "dev"), P("wa", None, "dev")),
        check_vma=False,
    )
```

```python
import functools

import jax
import jax.numpy as jnp
from jax import lax
from jax.sharding import PartitionSpec as P

TILE = 16
BF16 = jnp.bfloat16
F32 = jnp.float32

ROWS = (12, 13, 16)

PLAN = (
    ("a0", "y", 2),
    ("a1", "z", 6),
    ("a2", "y", 6),
    ("b0", "y", 2),
    ("b1", "y", 3),
    ("b2", "y", 3),
    ("b3", "y", 2),
    ("b4", "y", 2),
    ("b5", "z", 2),
    ("g", "y", 0),
)
EVENTS = (
    *("a0", "b5", "b1", "a0", "a1", "a0", "b0", "a2", "b1", "a1-", "a2", "b2"),
    *("b5", "a2", "b0", "b3", "b1", "b2", "b0", "b1", "b4", "b3", "b2", "b0"),
    *("g", "b4", "b3", "b2", "b5", "g", "b3", "b4", "b5", "a1", "g", "b4"),
    *("a1", "g"),
)


def nt_dot(left, right):
    return lax.dot_general(left, right, (((1,), (1,)), ((), ())), preferred_element_type=F32)


def tn_dot(left, right):
    return lax.dot_general(left, right, (((0,), (0,)), ((), ())), preferred_element_type=F32)


def nn_dot(left, right):
    return jnp.dot(left, right, preferred_element_type=F32)


def xor_permute(value, axis, size, distance):
    return lax.ppermute(value, axis, [(d, d ^ distance) for d in range(size)])


def ordered_offsets(bits):
    offsets = [0]
    for bit in reversed(bits):
        offsets = [o | bit for o in offsets] + offsets
    return offsets


class Lane:
    def __init__(self, chain):
        self.chain = chain
        self.result = None
        self.request = next(chain)
        self.send(self.request[0])

    def send(self, value):
        self.value = xor_permute(value, *self.request[1:])
        self.request = None

    def advance(self, value, hold):
        if self.request is not None:
            self.send(value)
            return
        try:
            self.request = self.chain.send(value)
            self.value = self.request[0]
            if not hold:
                self.send(self.value)
        except StopIteration as end:
            self.result = end.value


class Cell:
    def __init__(self, value):
        self.value = value


class Timeline:
    def __init__(self):
        self.cells = []
        self.renewed = []

    def prepare(self, value):
        cell = Cell(value)
        self.cells.append(cell)
        return cell

    def fence(self, *lanes, hold=False):
        cells, self.cells = self.cells + self.renewed, []
        leaves, tree = jax.tree.flatten(
            ([lane.value for lane in lanes], [cell.value for cell in cells])
        )
        values, prepared = jax.tree.unflatten(tree, lax.optimization_barrier(tuple(leaves)))
        for cell, value in zip(cells, prepared):
            cell.value = value
        for lane, value in zip(lanes, values):
            lane.advance(value, hold)


def single(value, size, distance):
    arrived = yield value, "wa", size, distance
    return arrived


def gather_dev(block, size, distances):
    held = block[None]
    for distance in distances:
        arrived = yield held, "dev", size, distance
        if distance != distances[-1]:
            held = jnp.concatenate([held, arrived], axis=0)
    return held, arrived


def sum_dev(value, size, distances):
    for distance in distances:
        arrived = yield value, "dev", size, distance
        value = value + arrived
    return value


def scatter_sum(away, kept, size, bits):
    for index, bit in enumerate(bits):
        arrived = yield away, "wa", size, bit
        total = kept.value.astype(F32) + arrived.astype(F32)
        if index + 1 < len(bits):
            half = total.shape[0] // 2
            total = total.astype(BF16)
            away, kept = total[:half], Cell(total[half:])
    return total


def packing(me, token_rows, tile_owner_adapter, tile_live_count):
    all_tiles = jnp.arange(tile_live_count.shape[0], dtype=jnp.int32)[:, None]
    row = jnp.arange(token_rows, dtype=jnp.int32)
    first_tile = me * (token_rows // TILE)
    tile_of_row = first_tile + row // TILE
    here = all_tiles == tile_of_row[None, :]
    before = (all_tiles >= first_tile) & (all_tiles < tile_of_row[None, :])
    live = jnp.sum(jnp.where(here, tile_live_count[:, None], 0), axis=0)
    begin = jnp.sum(jnp.where(before, tile_live_count[:, None], 0), axis=0)
    row_adapter = jnp.sum(jnp.where(here, tile_owner_adapter, 0), axis=0)
    position = row % TILE
    return jnp.where(position < live, begin + position, -1), row_adapter


def run(
    rows,
    wa_size,
    dev_size,
    output_gradient,
    down_weight,
    gate_preactivation,
    up_preactivation,
    adapter_down_factor,
    adapter_up_factor,
    tile_owner_adapter,
    tile_live_count,
):
    me = lax.axis_index("wa")
    dev = lax.axis_index("dev")
    token_rows = output_gradient.shape[0]
    hidden_local, group_width = down_weight.shape
    shard_columns = adapter_up_factor.shape[2]
    adapters, rank = adapter_down_factor.shape[:2]
    owned = adapters // wa_size
    sub_width = group_width // dev_size
    wa_bits = [1 << b for b in range(wa_size.bit_length() - 1)]
    dev_steps = [1 << b for b in reversed(range(dev_size.bit_length() - 1))]
    offsets = ordered_offsets(wa_bits)
    half = len(offsets) // 2
    time = Timeline()

    target, row_adapter = packing(me, token_rows, tile_owner_adapter, tile_live_count)
    pick = (jnp.arange(rows, dtype=jnp.int32)[:, None] == target[None, :]).astype(BF16)

    def compact(values):
        return nn_dot(pick, values).astype(BF16)

    flat_up = adapter_up_factor.reshape(adapters * rank, shard_columns)
    flat_down = adapter_down_factor.reshape(adapters * rank, hidden_local)

    def selector_for(order):
        return nn_dot(pick, (row_adapter[:, None] == order[None, :]).astype(BF16)).astype(BF16)

    selector = selector_for(jnp.arange(adapters, dtype=jnp.int32))

    def choose(values):
        wide = values.reshape(rows, adapters, rank) * selector.astype(F32)[:, :, None]
        return jnp.sum(wide, axis=1)

    def spread(values, which):
        wide = values[:, None, :] * which[:, :, None]
        return wide.reshape(rows, adapters * rank)

    def owner_spread(values, bits):
        place = jnp.arange(adapters, dtype=jnp.int32) // owned
        offset = sum(
            jnp.where((place >> (len(bits) - 1 - k)) & 1 == 0, bit, 0)
            for k, bit in enumerate(bits)
        )
        order = jnp.bitwise_xor(me, offset) * owned + jnp.arange(adapters, dtype=jnp.int32) % owned
        wide = spread(values, selector_for(order))
        middle = wide.shape[1] // 2
        return wide[:, :middle], wide[:, middle:]

    gradient = time.prepare(compact(output_gradient))
    time.fence()
    begins = [jnp.bitwise_xor(me, o) * group_width + dev * sub_width for o in offsets]
    pieces = [
        time.prepare(lax.dynamic_slice_in_dim(gradient.value, begin, sub_width, 1))
        for begin in begins
    ]
    steps = len(dev_steps)
    grad_slice = lax.dynamic_slice_in_dim(gradient.value, dev * shard_columns, shard_columns, 1)
    out_partial = time.prepare(choose(nt_dot(grad_slice, flat_up)))
    gate_all, up_all = time.prepare(gate_preactivation), time.prepare(up_preactivation)
    time.fence()
    out_lane = Lane(sum_dev(out_partial.value, dev_size, dev_steps))
    first_lanes = [Lane(single(pieces[k].value, wa_size, offsets[k])) for k in range(half)]
    gate = time.prepare(compact(gate_all.value))
    up = time.prepare(compact(up_all.value))
    hidden = time.prepare(
        (jax.nn.silu(gate.value.astype(F32)) * up.value.astype(F32)).astype(BF16)
    )
    time.fence(out_lane, *first_lanes)
    first = jnp.concatenate([lane.result for lane in first_lanes], axis=0)
    first_lane = Lane(gather_dev(first, dev_size, dev_steps))
    second_lanes = [
        Lane(single(pieces[k].value, wa_size, offsets[k])) for k in range(half, len(offsets) - 1)
    ]
    in_partial = time.prepare(choose(nt_dot(hidden.value, flat_down)))
    for _ in range(steps - 2):
        time.fence(out_lane)
    time.fence(out_lane, *second_lanes)
    lora_out = out_lane.result.astype(BF16)
    spread_out = time.prepare(spread(lora_out, selector))

    orders = {
        "y": wa_bits,
        "z": wa_bits[1:] + wa_bits[:1],
    }
    unit = hidden_local // 14
    kinds, spans, at = {}, {}, {"a": 0, "b": 0}
    for name, kind, width in PLAN:
        kinds[name] = orders[kind]
        begin = at.get(name[0], 0)
        spans[name] = slice(begin * unit, (begin + width) * unit)
        at[name[0]] = begin + width
    ready, lanes = {}, {}

    def ready_adapter(name, values, others):
        ready[name] = tuple(
            time.prepare(tn_dot(part, others).astype(BF16))
            for part in owner_spread(values, kinds[name])
        )

    def launch(name):
        away, own = ready[name]
        lanes[name] = Lane(scatter_sum(away.value, own, wa_size, kinds[name]))

    second = jnp.concatenate([lane.result for lane in second_lanes] + [pieces[-1].value], axis=0)
    second_lane = Lane(gather_dev(second, dev_size, dev_steps))
    in_lane = Lane(sum_dev(in_partial.value, dev_size, dev_steps))
    for name in ("a0", "a1"):
        ready_adapter(name, lora_out, hidden.value[:, spans[name]])
        launch(name)
    time.renewed = [hidden, spread_out]
    for _ in range(steps - 1):
        time.fence(first_lane, in_lane)
        time.fence(second_lane)
    ready_adapter("a2", lora_out, hidden.value[:, spans["a2"]])
    time.fence(in_lane)
    launch("a2")

    def assemble(lane):
        held, arrived = lane.result
        parts = []
        for j in range(dev_size):
            offset = jnp.bitwise_xor(dev, j)
            place = sum(
                ((offset >> (step.bit_length() - 1)) & 1) << k
                for k, step in enumerate(dev_steps[:-1])
            )
            near, far = (
                lax.dynamic_index_in_dim(x, place, 0, keepdims=False) for x in (held, arrived)
            )
            parts.append(jnp.where(offset & dev_steps[-1] == 0, near, far))
        return jnp.concatenate(parts, axis=1)

    columns_away, columns_own = Cell(None), Cell(None)

    def need_columns():
        if columns_away.value is None:
            time.fence(first_lane, second_lane)
            columns_away.value, columns_own.value = assemble(first_lane), assemble(second_lane)
            time.renewed += [columns_away, columns_own]

    def columns_for(bits):
        if bits == wa_bits:
            return columns_away.value, columns_own.value
        blocks = {}
        for k, offset in enumerate(offsets):
            part = columns_away.value if k < half else columns_own.value
            blocks[offset] = part[(k % half) * rows : (k % half + 1) * rows]
        order = [blocks[offset] for offset in ordered_offsets(bits)]
        return jnp.concatenate(order[:half], axis=0), jnp.concatenate(order[half:], axis=0)

    def make_ready(name):
        if name in ready:
            return
        if name == "g":
            ready_adapter(name, in_lane.result.astype(BF16), grad_slice)
            return
        if name[0] == "a":
            ready_adapter(name, lora_out, hidden.value[:, spans[name]])
            return
        need_columns()
        weights = down_weight[spans[name]]
        ready[name] = tuple(
            time.prepare(nt_dot(part, weights).astype(BF16)) for part in columns_for(kinds[name])
        )

    def finish(name):
        span = spans[name]
        hidden_grad = lanes[name].result + 2.0 * nn_dot(spread_out.value, flat_down[:, span])
        gate_here, up_here = gate.value[:, span].astype(F32), up.value[:, span].astype(F32)
        sigmoid = jax.nn.sigmoid(gate_here)
        grad_up = (hidden_grad * gate_here * sigmoid).astype(BF16)
        grad_gate = (
            hidden_grad * up_here * sigmoid * (1.0 + gate_here * (1.0 - sigmoid))
        ).astype(BF16)
        return time.prepare(
            (tn_dot(pick, grad_gate).astype(BF16), tn_dot(pick, grad_up).astype(BF16))
        )

    done = {}
    names = [event[:2].rstrip("-") for event in EVENTS]
    for index, name in enumerate(names):
        for soon in names[index : index + 3]:
            make_ready(soon)
        if name not in lanes:
            time.fence()
            launch(name)
            continue
        lane = lanes[name]
        time.fence(lane, hold=EVENTS[index].endswith("-"))
        while lane.result is None and name not in names[index + 1 :]:
            time.fence(lane)
        if lane.result is not None:
            done[name] = finish(name) if name[0] == "b" else Cell(2.0 * lane.result)

    def joined(letter, index=None):
        names = sorted(name for name in done if name[0] == letter)
        values = [done[name].value for name in names]
        return jnp.concatenate(values if index is None else [v[index] for v in values], axis=1)

    return (
        joined("b", 0),
        joined("b", 1),
        joined("a").reshape(owned, rank, hidden_local),
        joined("g").reshape(owned, rank, shard_columns),
    )


def solution(mesh):
    wa_size, dev_size = mesh.shape["wa"], mesh.shape["dev"]

    def on_device(*inputs):
        live = inputs[-1]
        sizes = [inputs[0].shape[0] * part // 16 for part in ROWS]
        tile = jnp.arange(live.shape[0], dtype=jnp.int32)[:, None]
        shard = jnp.arange(wa_size, dtype=jnp.int32)[None, :]
        here = tile // (live.shape[0] // wa_size) == shard
        totals = jnp.sum(jnp.where(here, live[:, None], 0), axis=0)
        above = sum((totals > size).astype(jnp.int32) for size in sizes[:-1])
        programs = [functools.partial(run, size, wa_size, dev_size) for size in sizes]
        return lax.switch(jnp.max(above), programs, *inputs)

    placed = (
        P("wa", None),
        P("dev", "wa"),
        P("wa", "dev"),
        P("wa", "dev"),
        P(None, None, "dev"),
        P(None, None, "dev"),
        P(),
        P(),
    )
    return jax.shard_map(
        on_device,
        mesh=mesh,
        in_specs=placed,
        out_specs=(P("wa", "dev"), P("wa", "dev"), P("wa", None, "dev"), P("wa", None, "dev")),
        check_vma=False,
    )
```

```python
import functools

import jax
import jax.numpy as jnp
from jax import lax
from jax.sharding import PartitionSpec as P

TILE = 16
BF16 = jnp.bfloat16
F32 = jnp.float32

ROWS = (12, 13, 16)

PLAN = (
    ("a0", "y", 2),
    ("a1", "z", 6),
    ("a2", "y", 6),
    ("b0", "y", 2),
    ("b1", "y", 3),
    ("b2", "y", 3),
    ("b3", "y", 2),
    ("b4", "y", 2),
    ("b5", "z", 2),
    ("g", "y", 0),
)
EVENTS = (
    *("b5", "b1", "a0", "a1", "a0", "b0", "a2", "b1", "a1-", "a2", "b2"),
    *("b5", "a2", "b0", "b3", "b1", "b2", "b0", "b1", "b4", "b3", "b2", "b0"),
    *("g", "b4", "b3", "b2", "b5", "g", "b3", "b4", "b5", "a1", "g", "b4"),
    *("a1", "g"),
)


def nt_dot(left, right):
    return lax.dot_general(left, right, (((1,), (1,)), ((), ())), preferred_element_type=F32)


def tn_dot(left, right):
    return lax.dot_general(left, right, (((0,), (0,)), ((), ())), preferred_element_type=F32)


def nn_dot(left, right):
    return jnp.dot(left, right, preferred_element_type=F32)


def xor_permute(value, axis, size, distance):
    return lax.ppermute(value, axis, [(d, d ^ distance) for d in range(size)])


def ordered_offsets(bits):
    offsets = [0]
    for bit in reversed(bits):
        offsets = [o | bit for o in offsets] + offsets
    return offsets


class Lane:
    def __init__(self, chain):
        self.chain = chain
        self.result = None
        self.request = next(chain)
        self.send(self.request[0])

    def send(self, value):
        self.value = xor_permute(value, *self.request[1:])
        self.request = None

    def advance(self, value, hold):
        if self.request is not None:
            self.send(value)
            return
        try:
            self.request = self.chain.send(value)
            self.value = self.request[0]
            if not hold:
                self.send(self.value)
        except StopIteration as end:
            self.result = end.value


class Cell:
    def __init__(self, value):
        self.value = value


class Timeline:
    def __init__(self):
        self.cells = []
        self.renewed = []

    def prepare(self, value):
        cell = Cell(value)
        self.cells.append(cell)
        return cell

    def fence(self, *lanes, hold=False):
        cells, self.cells = self.cells + self.renewed, []
        leaves, tree = jax.tree.flatten(
            ([lane.value for lane in lanes], [cell.value for cell in cells])
        )
        values, prepared = jax.tree.unflatten(tree, lax.optimization_barrier(tuple(leaves)))
        for cell, value in zip(cells, prepared):
            cell.value = value
        for lane, value in zip(lanes, values):
            lane.advance(value, hold)


def single(value, size, distance):
    arrived = yield value, "wa", size, distance
    return arrived


def gather_dev(block, size, distances):
    held = block[None]
    for distance in distances:
        arrived = yield held, "dev", size, distance
        if distance != distances[-1]:
            held = jnp.concatenate([held, arrived], axis=0)
    return held, arrived


def sum_dev(value, size, distances):
    for distance in distances:
        arrived = yield value, "dev", size, distance
        value = value + arrived
    return value


def scatter_sum(away, kept, size, bits):
    for index, bit in enumerate(bits):
        arrived = yield away, "wa", size, bit
        total = kept.value.astype(F32) + arrived.astype(F32)
        if index + 1 < len(bits):
            half = total.shape[0] // 2
            total = total.astype(BF16)
            away, kept = total[:half], Cell(total[half:])
    return total


def packing(me, token_rows, tile_owner_adapter, tile_live_count):
    all_tiles = jnp.arange(tile_live_count.shape[0], dtype=jnp.int32)[:, None]
    row = jnp.arange(token_rows, dtype=jnp.int32)
    first_tile = me * (token_rows // TILE)
    tile_of_row = first_tile + row // TILE
    here = all_tiles == tile_of_row[None, :]
    before = (all_tiles >= first_tile) & (all_tiles < tile_of_row[None, :])
    live = jnp.sum(jnp.where(here, tile_live_count[:, None], 0), axis=0)
    begin = jnp.sum(jnp.where(before, tile_live_count[:, None], 0), axis=0)
    row_adapter = jnp.sum(jnp.where(here, tile_owner_adapter, 0), axis=0)
    position = row % TILE
    return jnp.where(position < live, begin + position, -1), row_adapter


def run(
    rows,
    wa_size,
    dev_size,
    output_gradient,
    down_weight,
    gate_preactivation,
    up_preactivation,
    adapter_down_factor,
    adapter_up_factor,
    tile_owner_adapter,
    tile_live_count,
):
    me = lax.axis_index("wa")
    dev = lax.axis_index("dev")
    token_rows = output_gradient.shape[0]
    hidden_local, group_width = down_weight.shape
    shard_columns = adapter_up_factor.shape[2]
    adapters, rank = adapter_down_factor.shape[:2]
    owned = adapters // wa_size
    sub_width = group_width // dev_size
    wa_bits = [1 << b for b in range(wa_size.bit_length() - 1)]
    dev_steps = [1 << b for b in reversed(range(dev_size.bit_length() - 1))]
    offsets = ordered_offsets(wa_bits)
    half = len(offsets) // 2
    time = Timeline()

    target, row_adapter = packing(me, token_rows, tile_owner_adapter, tile_live_count)
    pick = (jnp.arange(rows, dtype=jnp.int32)[:, None] == target[None, :]).astype(BF16)

    def compact(values):
        return nn_dot(pick, values).astype(BF16)

    flat_up = adapter_up_factor.reshape(adapters * rank, shard_columns)
    flat_down = adapter_down_factor.reshape(adapters * rank, hidden_local)

    column = jnp.arange(adapters * rank, dtype=jnp.int32)
    unit_rank = jnp.arange(rank, dtype=jnp.int32)[:, None] == column[None, :] % rank

    def selector_for(owner):
        return nn_dot(pick, (row_adapter[:, None] == owner[None, :]).astype(BF16)).astype(BF16)

    selector = selector_for(column // rank)

    def choose(values):
        return lax.dot_general(
            values * selector.astype(F32),
            unit_rank.astype(F32),
            (((1,), (1,)), ((), ())),
            precision=lax.Precision.HIGHEST,
            preferred_element_type=F32,
        )

    def spread(values, which):
        return nn_dot(values, unit_rank.astype(BF16)).astype(BF16) * which

    def owner_spread(values, bits):
        place = column // (rank * owned)
        offset = sum(
            jnp.where((place >> (len(bits) - 1 - k)) & 1 == 0, bit, 0)
            for k, bit in enumerate(bits)
        )
        owner = jnp.bitwise_xor(me, offset) * owned + column // rank % owned
        wide = spread(values, selector_for(owner))
        middle = wide.shape[1] // 2
        return wide[:, :middle], wide[:, middle:]

    gradient = time.prepare(compact(output_gradient))
    time.fence()
    begins = [jnp.bitwise_xor(me, o) * group_width + dev * sub_width for o in offsets]
    pieces = [
        time.prepare(lax.dynamic_slice_in_dim(gradient.value, begin, sub_width, 1))
        for begin in begins
    ]
    steps = len(dev_steps)
    grad_slice = lax.dynamic_slice_in_dim(gradient.value, dev * shard_columns, shard_columns, 1)
    out_partial = time.prepare(choose(nt_dot(grad_slice, flat_up)))
    gate_all, up_all = time.prepare(gate_preactivation), time.prepare(up_preactivation)
    time.fence()
    out_lane = Lane(sum_dev(out_partial.value, dev_size, dev_steps))
    first_lanes = [Lane(single(pieces[k].value, wa_size, offsets[k])) for k in range(half)]
    gate = time.prepare(compact(gate_all.value))
    up = time.prepare(compact(up_all.value))
    hidden = time.prepare(
        (jax.nn.silu(gate.value.astype(F32)) * up.value.astype(F32)).astype(BF16)
    )
    for _ in range(steps):
        time.fence(out_lane)
    lora_out = out_lane.result.astype(BF16)
    spread_out = time.prepare(spread(lora_out, selector))
    time.renewed = [hidden, spread_out]

    orders = {
        "y": wa_bits,
        "z": wa_bits[1:] + wa_bits[:1],
    }
    unit = hidden_local // 14
    kinds, spans, at = {}, {}, {"a": 0, "b": 0}
    for name, kind, width in PLAN:
        kinds[name] = orders[kind]
        begin = at.get(name[0], 0)
        spans[name] = slice(begin * unit, (begin + width) * unit)
        at[name[0]] = begin + width
    ready, lanes = {}, {}

    def ready_adapter(name, values, others):
        ready[name] = tuple(
            time.prepare(tn_dot(part, others).astype(BF16))
            for part in owner_spread(values, kinds[name])
        )

    def launch(name):
        away, own = ready[name]
        lanes[name] = Lane(scatter_sum(away.value, own, wa_size, kinds[name]))

    ready_adapter("a0", lora_out, hidden.value[:, spans["a0"]])
    time.fence(*first_lanes)
    first = jnp.concatenate([lane.result for lane in first_lanes], axis=0)
    first_lane = Lane(gather_dev(first, dev_size, dev_steps))
    launch("a0")
    second_lanes = [
        Lane(single(pieces[k].value, wa_size, offsets[k])) for k in range(half, len(offsets) - 1)
    ]
    ready_adapter("a1", lora_out, hidden.value[:, spans["a1"]])
    in_partial = time.prepare(choose(nt_dot(hidden.value, flat_down)))
    ready_adapter("a2", lora_out, hidden.value[:, spans["a2"]])
    time.fence(*second_lanes, lanes["a0"])
    second = jnp.concatenate([lane.result for lane in second_lanes] + [pieces[-1].value], axis=0)
    second_lane = Lane(gather_dev(second, dev_size, dev_steps))
    launch("a1")
    launch("a2")
    for _ in range(steps - 1):
        time.fence(first_lane)
        time.fence(second_lane)
    in_lane = Lane(sum_dev(in_partial.value, dev_size, dev_steps))

    def assemble(lane):
        held, arrived = lane.result
        parts = []
        for j in range(dev_size):
            offset = jnp.bitwise_xor(dev, j)
            place = sum(
                ((offset >> (step.bit_length() - 1)) & 1) << k
                for k, step in enumerate(dev_steps[:-1])
            )
            near, far = (
                lax.dynamic_index_in_dim(x, place, 0, keepdims=False) for x in (held, arrived)
            )
            parts.append(jnp.where(offset & dev_steps[-1] == 0, near, far))
        return jnp.concatenate(parts, axis=1)

    columns_away, columns_own = Cell(None), Cell(None)

    def need_columns():
        if columns_away.value is None:
            time.fence(first_lane, second_lane, in_lane)
            for _ in range(steps - 1):
                time.fence(in_lane)
            columns_away.value, columns_own.value = assemble(first_lane), assemble(second_lane)
            time.renewed += [columns_away, columns_own]

    def columns_for(bits):
        if bits == wa_bits:
            return columns_away.value, columns_own.value
        blocks = {}
        for k, offset in enumerate(offsets):
            part = columns_away.value if k < half else columns_own.value
            blocks[offset] = part[(k % half) * rows : (k % half + 1) * rows]
        order = [blocks[offset] for offset in ordered_offsets(bits)]
        return jnp.concatenate(order[:half], axis=0), jnp.concatenate(order[half:], axis=0)

    def make_ready(name):
        if name in ready:
            return
        if name == "g":
            ready_adapter(name, in_lane.result.astype(BF16), grad_slice)
            return
        if name[0] == "a":
            ready_adapter(name, lora_out, hidden.value[:, spans[name]])
            return
        need_columns()
        weights = down_weight[spans[name]]
        ready[name] = tuple(
            time.prepare(nt_dot(part, weights).astype(BF16)) for part in columns_for(kinds[name])
        )

    def finish(name):
        span = spans[name]
        hidden_grad = lanes[name].result + 2.0 * nn_dot(spread_out.value, flat_down[:, span])
        gate_here, up_here = gate.value[:, span].astype(F32), up.value[:, span].astype(F32)
        sigmoid = jax.nn.sigmoid(gate_here)
        grad_up = (hidden_grad * gate_here * sigmoid).astype(BF16)
        grad_gate = (
            hidden_grad * up_here * sigmoid * (1.0 + gate_here * (1.0 - sigmoid))
        ).astype(BF16)
        return time.prepare(
            (tn_dot(pick, grad_gate).astype(BF16), tn_dot(pick, grad_up).astype(BF16))
        )

    done = {}
    names = [event[:2].rstrip("-") for event in EVENTS]
    for index, name in enumerate(names):
        for soon in names[index : index + 3]:
            make_ready(soon)
        if name not in lanes:
            time.fence()
            launch(name)
            continue
        lane = lanes[name]
        time.fence(lane, hold=EVENTS[index].endswith("-"))
        while lane.result is None and name not in names[index + 1 :]:
            time.fence(lane)
        if lane.result is not None:
            done[name] = finish(name) if name[0] == "b" else Cell(2.0 * lane.result)

    def joined(letter, index=None):
        names = sorted(name for name in done if name[0] == letter)
        values = [done[name].value for name in names]
        return jnp.concatenate(values if index is None else [v[index] for v in values], axis=1)

    return (
        joined("b", 0),
        joined("b", 1),
        joined("a").reshape(owned, rank, hidden_local),
        joined("g").reshape(owned, rank, shard_columns),
    )


def solution(mesh):
    wa_size, dev_size = mesh.shape["wa"], mesh.shape["dev"]

    def on_device(*inputs):
        live = inputs[-1]
        sizes = [inputs[0].shape[0] * part // 16 for part in ROWS]
        tile = jnp.arange(live.shape[0], dtype=jnp.int32)[:, None]
        shard = jnp.arange(wa_size, dtype=jnp.int32)[None, :]
        here = tile // (live.shape[0] // wa_size) == shard
        totals = jnp.sum(jnp.where(here, live[:, None], 0), axis=0)
        above = sum((totals > size).astype(jnp.int32) for size in sizes[:-1])
        programs = [functools.partial(run, size, wa_size, dev_size) for size in sizes]
        return lax.switch(jnp.max(above), programs, *inputs)

    placed = (
        P("wa", None),
        P("dev", "wa"),
        P("wa", "dev"),
        P("wa", "dev"),
        P(None, None, "dev"),
        P(None, None, "dev"),
        P(),
        P(),
    )
    return jax.shard_map(
        on_device,
        mesh=mesh,
        in_specs=placed,
        out_specs=(P("wa", "dev"), P("wa", "dev"), P("wa", None, "dev"), P("wa", None, "dev")),
        check_vma=False,
    )
```

```python
import functools

import jax
import jax.numpy as jnp
from jax import lax
from jax.sharding import PartitionSpec as P

TILE = 16
BF16 = jnp.bfloat16
F32 = jnp.float32

ROWS = (12, 13, 16)

PLAN = (
    ("a0", "y", 4),
    ("a1", "z", 5),
    ("a2", "y", 5),
    ("b0", "y", 2),
    ("b1", "y", 3),
    ("b2", "y", 3),
    ("b3", "y", 2),
    ("b4", "y", 2),
    ("b5", "z", 2),
    ("g", "y", 0),
)
EVENTS = (
    *("a0", "b5", "b1", "a0", "a1", "a2", "a0", "b0", "b1", "a1-", "a2", "b2"),
    *("b5", "b0", "a2", "b3", "b1", "b2", "b1", "b0", "b4", "b3", "b2", "b0"),
    *("g", "b4", "b3", "b2", "g-", "g", "b5", "a1", "b4", "b5", "a1", "g"),
    *("b3", "b4", "g"),
)


def nt_dot(left, right):
    return lax.dot_general(left, right, (((1,), (1,)), ((), ())), preferred_element_type=F32)


def tn_dot(left, right):
    return lax.dot_general(left, right, (((0,), (0,)), ((), ())), preferred_element_type=F32)


def nn_dot(left, right):
    return jnp.dot(left, right, preferred_element_type=F32)


def xor_permute(value, axis, size, distance):
    return lax.ppermute(value, axis, [(d, d ^ distance) for d in range(size)])


def ordered_offsets(bits):
    offsets = [0]
    for bit in reversed(bits):
        offsets = [o | bit for o in offsets] + offsets
    return offsets


class Lane:
    def __init__(self, chain):
        self.chain = chain
        self.result = None
        self.request = next(chain)
        self.send(self.request[0])

    def send(self, value):
        self.value = xor_permute(value, *self.request[1:])
        self.request = None

    def advance(self, value, hold):
        if self.request is not None:
            self.send(value)
            return
        try:
            self.request = self.chain.send(value)
            self.value = self.request[0]
            if not hold:
                self.send(self.value)
        except StopIteration as end:
            self.result = end.value


class Cell:
    def __init__(self, value):
        self.value = value


class Timeline:
    def __init__(self):
        self.cells = []
        self.renewed = []

    def prepare(self, value):
        cell = Cell(value)
        self.cells.append(cell)
        return cell

    def fence(self, *lanes, hold=False):
        cells, self.cells = self.cells + self.renewed, []
        leaves, tree = jax.tree.flatten(
            ([lane.value for lane in lanes], [cell.value for cell in cells])
        )
        values, prepared = jax.tree.unflatten(tree, lax.optimization_barrier(tuple(leaves)))
        for cell, value in zip(cells, prepared):
            cell.value = value
        for lane, value in zip(lanes, values):
            lane.advance(value, hold)


def single(value, size, distance):
    arrived = yield value, "wa", size, distance
    return arrived


def gather_dev(block, size, distances):
    held = block[None]
    for distance in distances:
        arrived = yield held, "dev", size, distance
        if distance != distances[-1]:
            held = jnp.concatenate([held, arrived], axis=0)
    return held, arrived


def sum_dev(value, size, distances):
    for distance in distances:
        arrived = yield value, "dev", size, distance
        value = value + arrived
    return value


def scatter_sum(away, kept, size, bits):
    for index, bit in enumerate(bits):
        arrived = yield away, "wa", size, bit
        total = kept.value.astype(F32) + arrived.astype(F32)
        if index + 1 < len(bits):
            half = total.shape[0] // 2
            total = total.astype(BF16)
            away, kept = total[:half], Cell(total[half:])
    return total


def packing(me, token_rows, tile_owner_adapter, tile_live_count):
    all_tiles = jnp.arange(tile_live_count.shape[0], dtype=jnp.int32)[:, None]
    row = jnp.arange(token_rows, dtype=jnp.int32)
    first_tile = me * (token_rows // TILE)
    tile_of_row = first_tile + row // TILE
    here = all_tiles == tile_of_row[None, :]
    before = (all_tiles >= first_tile) & (all_tiles < tile_of_row[None, :])
    live = jnp.sum(jnp.where(here, tile_live_count[:, None], 0), axis=0)
    begin = jnp.sum(jnp.where(before, tile_live_count[:, None], 0), axis=0)
    row_adapter = jnp.sum(jnp.where(here, tile_owner_adapter, 0), axis=0)
    position = row % TILE
    return jnp.where(position < live, begin + position, -1), row_adapter


def run(
    rows,
    wa_size,
    dev_size,
    output_gradient,
    down_weight,
    gate_preactivation,
    up_preactivation,
    adapter_down_factor,
    adapter_up_factor,
    tile_owner_adapter,
    tile_live_count,
):
    me = lax.axis_index("wa")
    dev = lax.axis_index("dev")
    token_rows = output_gradient.shape[0]
    hidden_local, group_width = down_weight.shape
    shard_columns = adapter_up_factor.shape[2]
    adapters, rank = adapter_down_factor.shape[:2]
    owned = adapters // wa_size
    sub_width = group_width // dev_size
    wa_bits = [1 << b for b in range(wa_size.bit_length() - 1)]
    dev_steps = [1 << b for b in reversed(range(dev_size.bit_length() - 1))]
    offsets = ordered_offsets(wa_bits)
    half = len(offsets) // 2
    time = Timeline()

    target, row_adapter = packing(me, token_rows, tile_owner_adapter, tile_live_count)
    pick = (jnp.arange(rows, dtype=jnp.int32)[:, None] == target[None, :]).astype(BF16)

    def compact(values):
        return nn_dot(pick, values).astype(BF16)

    flat_up = adapter_up_factor.reshape(adapters * rank, shard_columns)
    flat_down = adapter_down_factor.reshape(adapters * rank, hidden_local)

    def selector_for(order):
        return nn_dot(pick, (row_adapter[:, None] == order[None, :]).astype(BF16)).astype(BF16)

    selector = selector_for(jnp.arange(adapters, dtype=jnp.int32))

    def choose(values):
        wide = values.reshape(rows, adapters, rank) * selector.astype(F32)[:, :, None]
        return jnp.sum(wide, axis=1)

    def spread(values, which):
        wide = values[:, None, :] * which[:, :, None]
        return wide.reshape(rows, adapters * rank)

    def owner_spread(values, bits):
        place = jnp.arange(adapters, dtype=jnp.int32) // owned
        offset = sum(
            jnp.where((place >> (len(bits) - 1 - k)) & 1 == 0, bit, 0)
            for k, bit in enumerate(bits)
        )
        order = jnp.bitwise_xor(me, offset) * owned + jnp.arange(adapters, dtype=jnp.int32) % owned
        wide = spread(values, selector_for(order))
        middle = wide.shape[1] // 2
        return wide[:, :middle], wide[:, middle:]

    gradient = time.prepare(compact(output_gradient))
    time.fence()
    begins = [jnp.bitwise_xor(me, o) * group_width + dev * sub_width for o in offsets]
    pieces = [
        time.prepare(lax.dynamic_slice_in_dim(gradient.value, begin, sub_width, 1))
        for begin in begins
    ]
    steps = len(dev_steps)
    grad_slice = lax.dynamic_slice_in_dim(gradient.value, dev * shard_columns, shard_columns, 1)
    out_partial = time.prepare(choose(nt_dot(grad_slice, flat_up)))
    gate_all, up_all = time.prepare(gate_preactivation), time.prepare(up_preactivation)
    time.fence()
    out_lane = Lane(sum_dev(out_partial.value, dev_size, dev_steps))
    first_lanes = [Lane(single(pieces[k].value, wa_size, offsets[k])) for k in range(half)]
    gate = time.prepare(compact(gate_all.value))
    up = time.prepare(compact(up_all.value))
    hidden = time.prepare(
        (jax.nn.silu(gate.value.astype(F32)) * up.value.astype(F32)).astype(BF16)
    )
    time.fence(out_lane, *first_lanes)
    first = jnp.concatenate([lane.result for lane in first_lanes], axis=0)
    first_lane = Lane(gather_dev(first, dev_size, dev_steps))
    second_lanes = [
        Lane(single(pieces[k].value, wa_size, offsets[k])) for k in range(half, len(offsets) - 1)
    ]
    in_partial = time.prepare(choose(nt_dot(hidden.value, flat_down)))
    for _ in range(steps - 2):
        time.fence(out_lane)
    time.fence(out_lane, *second_lanes)
    lora_out = out_lane.result.astype(BF16)
    spread_out = time.prepare(spread(lora_out, selector))

    orders = {
        "y": wa_bits,
        "z": wa_bits[1:] + wa_bits[:1],
    }
    unit = hidden_local // 14
    kinds, spans, at = {}, {}, {"a": 0, "b": 0}
    for name, kind, width in PLAN:
        kinds[name] = orders[kind]
        begin = at.get(name[0], 0)
        spans[name] = slice(begin * unit, (begin + width) * unit)
        at[name[0]] = begin + width
    ready, lanes = {}, {}

    def ready_adapter(name, values, others):
        ready[name] = tuple(
            time.prepare(tn_dot(part, others).astype(BF16))
            for part in owner_spread(values, kinds[name])
        )

    def launch(name):
        away, own = ready[name]
        lanes[name] = Lane(scatter_sum(away.value, own, wa_size, kinds[name]))

    second = jnp.concatenate([lane.result for lane in second_lanes] + [pieces[-1].value], axis=0)
    second_lane = Lane(gather_dev(second, dev_size, dev_steps))
    in_lane = Lane(sum_dev(in_partial.value, dev_size, dev_steps))
    for name in ("a0", "a1"):
        ready_adapter(name, lora_out, hidden.value[:, spans[name]])
        launch(name)
    time.renewed = [hidden, spread_out]
    for _ in range(steps - 1):
        time.fence(first_lane, in_lane)
        time.fence(second_lane)
    ready_adapter("a2", lora_out, hidden.value[:, spans["a2"]])
    time.fence(in_lane)
    launch("a2")

    def assemble(lane):
        held, arrived = lane.result
        parts = []
        for j in range(dev_size):
            offset = jnp.bitwise_xor(dev, j)
            place = sum(
                ((offset >> (step.bit_length() - 1)) & 1) << k
                for k, step in enumerate(dev_steps[:-1])
            )
            near, far = (
                lax.dynamic_index_in_dim(x, place, 0, keepdims=False) for x in (held, arrived)
            )
            parts.append(jnp.where(offset & dev_steps[-1] == 0, near, far))
        return jnp.concatenate(parts, axis=1)

    columns_away, columns_own = Cell(None), Cell(None)

    def need_columns():
        if columns_away.value is None:
            time.fence(first_lane, second_lane)
            columns_away.value, columns_own.value = assemble(first_lane), assemble(second_lane)
            time.renewed += [columns_away, columns_own]

    def columns_for(bits):
        if bits == wa_bits:
            return columns_away.value, columns_own.value
        blocks = {}
        for k, offset in enumerate(offsets):
            part = columns_away.value if k < half else columns_own.value
            blocks[offset] = part[(k % half) * rows : (k % half + 1) * rows]
        order = [blocks[offset] for offset in ordered_offsets(bits)]
        return jnp.concatenate(order[:half], axis=0), jnp.concatenate(order[half:], axis=0)

    def make_ready(name):
        if name in ready:
            return
        if name == "g":
            ready_adapter(name, in_lane.result.astype(BF16), grad_slice)
            return
        if name[0] == "a":
            ready_adapter(name, lora_out, hidden.value[:, spans[name]])
            return
        need_columns()
        weights = down_weight[spans[name]]
        ready[name] = tuple(
            time.prepare(nt_dot(part, weights).astype(BF16)) for part in columns_for(kinds[name])
        )

    def finish(name):
        span = spans[name]
        hidden_grad = lanes[name].result + 2.0 * nn_dot(spread_out.value, flat_down[:, span])
        gate_here, up_here = gate.value[:, span].astype(F32), up.value[:, span].astype(F32)
        sigmoid = jax.nn.sigmoid(gate_here)
        grad_up = (hidden_grad * gate_here * sigmoid).astype(BF16)
        grad_gate = (
            hidden_grad * up_here * sigmoid * (1.0 + gate_here * (1.0 - sigmoid))
        ).astype(BF16)
        return time.prepare(
            (tn_dot(pick, grad_gate).astype(BF16), tn_dot(pick, grad_up).astype(BF16))
        )

    done = {}
    names = [event[:2].rstrip("-") for event in EVENTS]
    for index, name in enumerate(names):
        for soon in names[index : index + 3]:
            make_ready(soon)
        if name not in lanes:
            time.fence()
            launch(name)
            continue
        lane = lanes[name]
        time.fence(lane, hold=EVENTS[index].endswith("-"))
        while lane.result is None and name not in names[index + 1 :]:
            time.fence(lane)
        if lane.result is not None:
            done[name] = finish(name) if name[0] == "b" else Cell(2.0 * lane.result)

    def joined(letter, index=None):
        names = sorted(name for name in done if name[0] == letter)
        values = [done[name].value for name in names]
        return jnp.concatenate(values if index is None else [v[index] for v in values], axis=1)

    return (
        joined("b", 0),
        joined("b", 1),
        joined("a").reshape(owned, rank, hidden_local),
        joined("g").reshape(owned, rank, shard_columns),
    )


def solution(mesh):
    wa_size, dev_size = mesh.shape["wa"], mesh.shape["dev"]

    def on_device(*inputs):
        live = inputs[-1]
        sizes = [inputs[0].shape[0] * part // 16 for part in ROWS]
        tile = jnp.arange(live.shape[0], dtype=jnp.int32)[:, None]
        shard = jnp.arange(wa_size, dtype=jnp.int32)[None, :]
        here = tile // (live.shape[0] // wa_size) == shard
        totals = jnp.sum(jnp.where(here, live[:, None], 0), axis=0)
        above = sum((totals > size).astype(jnp.int32) for size in sizes[:-1])
        programs = [functools.partial(run, size, wa_size, dev_size) for size in sizes]
        return lax.switch(jnp.max(above), programs, *inputs)

    placed = (
        P("wa", None),
        P("dev", "wa"),
        P("wa", "dev"),
        P("wa", "dev"),
        P(None, None, "dev"),
        P(None, None, "dev"),
        P(),
        P(),
    )
    return jax.shard_map(
        on_device,
        mesh=mesh,
        in_specs=placed,
        out_specs=(P("wa", "dev"), P("wa", "dev"), P("wa", None, "dev"), P("wa", None, "dev")),
        check_vma=False,
    )
```

```python
import functools

import jax
import jax.numpy as jnp
from jax import lax
from jax.sharding import PartitionSpec as P

TILE = 16
BF16 = jnp.bfloat16
F32 = jnp.float32

ROWS = (11, 12, 13, 16)

PLAN = (
    ("a0", "y", 2),
    ("a1", "z", 6),
    ("a2", "y", 6),
    ("b0", "y", 2),
    ("b1", "y", 3),
    ("b2", "y", 3),
    ("b3", "y", 2),
    ("b4", "y", 2),
    ("b5", "z", 2),
    ("g", "y", 0),
)
EVENTS = (
    *("a0", "b5", "b1", "a0", "a1", "a0", "b0", "a2", "b1", "a1-", "a2", "b2"),
    *("b5", "a2", "b0", "b3", "b1", "b2", "b0", "b1", "b4", "b3", "b2", "b0"),
    *("g", "b4", "b3", "b2", "b5", "g", "b3", "b4", "b5", "a1", "g", "b4"),
    *("a1", "g"),
)


def nt_dot(left, right):
    return lax.dot_general(left, right, (((1,), (1,)), ((), ())), preferred_element_type=F32)


def tn_dot(left, right):
    return lax.dot_general(left, right, (((0,), (0,)), ((), ())), preferred_element_type=F32)


def nn_dot(left, right):
    return jnp.dot(left, right, preferred_element_type=F32)


def xor_permute(value, axis, size, distance):
    return lax.ppermute(value, axis, [(d, d ^ distance) for d in range(size)])


def ordered_offsets(bits):
    offsets = [0]
    for bit in reversed(bits):
        offsets = [o | bit for o in offsets] + offsets
    return offsets


class Lane:
    def __init__(self, chain):
        self.chain = chain
        self.result = None
        self.request = next(chain)
        self.send(self.request[0])

    def send(self, value):
        self.value = xor_permute(value, *self.request[1:])
        self.request = None

    def advance(self, value, hold):
        if self.request is not None:
            self.send(value)
            return
        try:
            self.request = self.chain.send(value)
            self.value = self.request[0]
            if not hold:
                self.send(self.value)
        except StopIteration as end:
            self.result = end.value


class Cell:
    def __init__(self, value):
        self.value = value


class Timeline:
    def __init__(self):
        self.cells = []
        self.renewed = []

    def prepare(self, value):
        cell = Cell(value)
        self.cells.append(cell)
        return cell

    def fence(self, *lanes, hold=False):
        cells, self.cells = self.cells + self.renewed, []
        leaves, tree = jax.tree.flatten(
            ([lane.value for lane in lanes], [cell.value for cell in cells])
        )
        values, prepared = jax.tree.unflatten(tree, lax.optimization_barrier(tuple(leaves)))
        for cell, value in zip(cells, prepared):
            cell.value = value
        for lane, value in zip(lanes, values):
            lane.advance(value, hold)


def single(value, size, distance):
    arrived = yield value, "wa", size, distance
    return arrived


def gather_dev(block, size, distances):
    held = block[None]
    for distance in distances:
        arrived = yield held, "dev", size, distance
        if distance != distances[-1]:
            held = jnp.concatenate([held, arrived], axis=0)
    return held, arrived


def sum_dev(value, size, distances):
    for distance in distances:
        arrived = yield value, "dev", size, distance
        value = value + arrived
    return value


def scatter_sum(away, kept, size, bits):
    for index, bit in enumerate(bits):
        arrived = yield away, "wa", size, bit
        total = kept.value.astype(F32) + arrived.astype(F32)
        if index + 1 < len(bits):
            half = total.shape[0] // 2
            total = total.astype(BF16)
            away, kept = total[:half], Cell(total[half:])
    return total


def packing(me, token_rows, tile_owner_adapter, tile_live_count):
    all_tiles = jnp.arange(tile_live_count.shape[0], dtype=jnp.int32)[:, None]
    row = jnp.arange(token_rows, dtype=jnp.int32)
    first_tile = me * (token_rows // TILE)
    tile_of_row = first_tile + row // TILE
    here = all_tiles == tile_of_row[None, :]
    before = (all_tiles >= first_tile) & (all_tiles < tile_of_row[None, :])
    live = jnp.sum(jnp.where(here, tile_live_count[:, None], 0), axis=0)
    begin = jnp.sum(jnp.where(before, tile_live_count[:, None], 0), axis=0)
    row_adapter = jnp.sum(jnp.where(here, tile_owner_adapter, 0), axis=0)
    position = row % TILE
    return jnp.where(position < live, begin + position, -1), row_adapter


def run(
    rows,
    wa_size,
    dev_size,
    output_gradient,
    down_weight,
    gate_preactivation,
    up_preactivation,
    adapter_down_factor,
    adapter_up_factor,
    tile_owner_adapter,
    tile_live_count,
):
    me = lax.axis_index("wa")
    dev = lax.axis_index("dev")
    token_rows = output_gradient.shape[0]
    hidden_local, group_width = down_weight.shape
    shard_columns = adapter_up_factor.shape[2]
    adapters, rank = adapter_down_factor.shape[:2]
    owned = adapters // wa_size
    sub_width = group_width // dev_size
    wa_bits = [1 << b for b in range(wa_size.bit_length() - 1)]
    dev_steps = [1 << b for b in reversed(range(dev_size.bit_length() - 1))]
    offsets = ordered_offsets(wa_bits)
    half = len(offsets) // 2
    time = Timeline()

    target, row_adapter = packing(me, token_rows, tile_owner_adapter, tile_live_count)
    pick = (jnp.arange(rows, dtype=jnp.int32)[:, None] == target[None, :]).astype(BF16)

    def compact(values):
        return nn_dot(pick, values).astype(BF16)

    flat_up = adapter_up_factor.reshape(adapters * rank, shard_columns)
    flat_down = adapter_down_factor.reshape(adapters * rank, hidden_local)

    def selector_for(order):
        return nn_dot(pick, (row_adapter[:, None] == order[None, :]).astype(BF16)).astype(BF16)

    selector = selector_for(jnp.arange(adapters, dtype=jnp.int32))

    def choose(values):
        wide = values.reshape(rows, adapters, rank) * selector.astype(F32)[:, :, None]
        return jnp.sum(wide, axis=1)

    def spread(values, which):
        wide = values[:, None, :] * which[:, :, None]
        return wide.reshape(rows, adapters * rank)

    def owner_spread(values, bits):
        place = jnp.arange(adapters, dtype=jnp.int32) // owned
        offset = sum(
            jnp.where((place >> (len(bits) - 1 - k)) & 1 == 0, bit, 0)
            for k, bit in enumerate(bits)
        )
        order = jnp.bitwise_xor(me, offset) * owned + jnp.arange(adapters, dtype=jnp.int32) % owned
        wide = spread(values, selector_for(order))
        middle = wide.shape[1] // 2
        return wide[:, :middle], wide[:, middle:]

    gradient = time.prepare(compact(output_gradient))
    time.fence()
    begins = [jnp.bitwise_xor(me, o) * group_width + dev * sub_width for o in offsets]
    pieces = [
        time.prepare(lax.dynamic_slice_in_dim(gradient.value, begin, sub_width, 1))
        for begin in begins
    ]
    steps = len(dev_steps)
    grad_slice = lax.dynamic_slice_in_dim(gradient.value, dev * shard_columns, shard_columns, 1)
    out_partial = time.prepare(choose(nt_dot(grad_slice, flat_up)))
    gate_all, up_all = time.prepare(gate_preactivation), time.prepare(up_preactivation)
    time.fence()
    out_lane = Lane(sum_dev(out_partial.value, dev_size, dev_steps))
    first_lanes = [Lane(single(pieces[k].value, wa_size, offsets[k])) for k in range(half)]
    gate = time.prepare(compact(gate_all.value))
    up = time.prepare(compact(up_all.value))
    hidden = time.prepare(
        (jax.nn.silu(gate.value.astype(F32)) * up.value.astype(F32)).astype(BF16)
    )
    time.fence(out_lane, *first_lanes)
    first = jnp.concatenate([lane.result for lane in first_lanes], axis=0)
    first_lane = Lane(gather_dev(first, dev_size, dev_steps))
    second_lanes = [
        Lane(single(pieces[k].value, wa_size, offsets[k])) for k in range(half, len(offsets) - 1)
    ]
    in_partial = time.prepare(choose(nt_dot(hidden.value, flat_down)))
    for _ in range(steps - 2):
        time.fence(out_lane)
    time.fence(out_lane, *second_lanes)
    lora_out = out_lane.result.astype(BF16)
    spread_out = time.prepare(spread(lora_out, selector))

    orders = {
        "y": wa_bits,
        "z": wa_bits[1:] + wa_bits[:1],
    }
    unit = hidden_local // 14
    kinds, spans, at = {}, {}, {"a": 0, "b": 0}
    for name, kind, width in PLAN:
        kinds[name] = orders[kind]
        begin = at.get(name[0], 0)
        spans[name] = slice(begin * unit, (begin + width) * unit)
        at[name[0]] = begin + width
    ready, lanes = {}, {}

    def ready_adapter(name, values, others):
        ready[name] = tuple(
            time.prepare(tn_dot(part, others).astype(BF16))
            for part in owner_spread(values, kinds[name])
        )

    def launch(name):
        away, own = ready[name]
        lanes[name] = Lane(scatter_sum(away.value, own, wa_size, kinds[name]))

    second = jnp.concatenate([lane.result for lane in second_lanes] + [pieces[-1].value], axis=0)
    second_lane = Lane(gather_dev(second, dev_size, dev_steps))
    in_lane = Lane(sum_dev(in_partial.value, dev_size, dev_steps))
    for name in ("a0", "a1"):
        ready_adapter(name, lora_out, hidden.value[:, spans[name]])
        launch(name)
    time.renewed = [hidden, spread_out]
    for _ in range(steps - 1):
        time.fence(first_lane, in_lane)
        time.fence(second_lane)
    ready_adapter("a2", lora_out, hidden.value[:, spans["a2"]])
    time.fence(in_lane)
    launch("a2")

    def assemble(lane):
        held, arrived = lane.result
        parts = []
        for j in range(dev_size):
            offset = jnp.bitwise_xor(dev, j)
            place = sum(
                ((offset >> (step.bit_length() - 1)) & 1) << k
                for k, step in enumerate(dev_steps[:-1])
            )
            near, far = (
                lax.dynamic_index_in_dim(x, place, 0, keepdims=False) for x in (held, arrived)
            )
            parts.append(jnp.where(offset & dev_steps[-1] == 0, near, far))
        return jnp.concatenate(parts, axis=1)

    columns_away, columns_own = Cell(None), Cell(None)

    def need_columns():
        if columns_away.value is None:
            time.fence(first_lane, second_lane)
            columns_away.value, columns_own.value = assemble(first_lane), assemble(second_lane)
            time.renewed += [columns_away, columns_own]

    def columns_for(bits):
        if bits == wa_bits:
            return columns_away.value, columns_own.value
        blocks = {}
        for k, offset in enumerate(offsets):
            part = columns_away.value if k < half else columns_own.value
            blocks[offset] = part[(k % half) * rows : (k % half + 1) * rows]
        order = [blocks[offset] for offset in ordered_offsets(bits)]
        return jnp.concatenate(order[:half], axis=0), jnp.concatenate(order[half:], axis=0)

    def make_ready(name):
        if name in ready:
            return
        if name == "g":
            ready_adapter(name, in_lane.result.astype(BF16), grad_slice)
            return
        if name[0] == "a":
            ready_adapter(name, lora_out, hidden.value[:, spans[name]])
            return
        need_columns()
        weights = down_weight[spans[name]]
        ready[name] = tuple(
            time.prepare(nt_dot(part, weights).astype(BF16)) for part in columns_for(kinds[name])
        )

    def finish(name):
        span = spans[name]
        hidden_grad = lanes[name].result + 2.0 * nn_dot(spread_out.value, flat_down[:, span])
        gate_here, up_here = gate.value[:, span].astype(F32), up.value[:, span].astype(F32)
        sigmoid = jax.nn.sigmoid(gate_here)
        grad_up = (hidden_grad * gate_here * sigmoid).astype(BF16)
        grad_gate = (
            hidden_grad * up_here * sigmoid * (1.0 + gate_here * (1.0 - sigmoid))
        ).astype(BF16)
        return time.prepare(
            (tn_dot(pick, grad_gate).astype(BF16), tn_dot(pick, grad_up).astype(BF16))
        )

    done = {}
    names = [event[:2].rstrip("-") for event in EVENTS]
    for index, name in enumerate(names):
        for soon in names[index : index + 3]:
            make_ready(soon)
        if name not in lanes:
            time.fence()
            launch(name)
            continue
        lane = lanes[name]
        time.fence(lane, hold=EVENTS[index].endswith("-"))
        while lane.result is None and name not in names[index + 1 :]:
            time.fence(lane)
        if lane.result is not None:
            done[name] = finish(name) if name[0] == "b" else Cell(2.0 * lane.result)

    def joined(letter, index=None):
        names = sorted(name for name in done if name[0] == letter)
        values = [done[name].value for name in names]
        return jnp.concatenate(values if index is None else [v[index] for v in values], axis=1)

    return (
        joined("b", 0),
        joined("b", 1),
        joined("a").reshape(owned, rank, hidden_local),
        joined("g").reshape(owned, rank, shard_columns),
    )


def solution(mesh):
    wa_size, dev_size = mesh.shape["wa"], mesh.shape["dev"]

    def on_device(*inputs):
        live = inputs[-1]
        sizes = [inputs[0].shape[0] * part // 16 for part in ROWS]
        tile = jnp.arange(live.shape[0], dtype=jnp.int32)[:, None]
        shard = jnp.arange(wa_size, dtype=jnp.int32)[None, :]
        here = tile // (live.shape[0] // wa_size) == shard
        totals = jnp.sum(jnp.where(here, live[:, None], 0), axis=0)
        above = sum((totals > size).astype(jnp.int32) for size in sizes[:-1])
        programs = [functools.partial(run, size, wa_size, dev_size) for size in sizes]
        return lax.switch(jnp.max(above), programs, *inputs)

    placed = (
        P("wa", None),
        P("dev", "wa"),
        P("wa", "dev"),
        P("wa", "dev"),
        P(None, None, "dev"),
        P(None, None, "dev"),
        P(),
        P(),
    )
    return jax.shard_map(
        on_device,
        mesh=mesh,
        in_specs=placed,
        out_specs=(P("wa", "dev"), P("wa", "dev"), P("wa", None, "dev"), P("wa", None, "dev")),
        check_vma=False,
    )
```
